32 devices in a mesh: tile: 16 (over z, y, x), mode: 2 (over core).
Axes of the slice: x: 2, y: 2, z: 4, core: 2. Of those that a mesh axis runs over, the one named last changes fastest.
Arguments:
- object_wave: float32 [2, 2048, 1024], P(None, 'tile'), may hold values from -6 to 6
- probe: float32 [2, 2, 128, 128], P('mode'), may hold values from -2 to 2
- amplitudes: bfloat16 [256, 128, 128], P('tile'), may hold values from 0.25 to 2.5
- row_offsets: int32 [256], P('tile'), may hold values from 0 to 128
- column_offsets: int32 [256], P('tile'), may hold values from 0 to 896
Outputs:
- object_grad: float32 [2, 2048, 1024], P(None, 'tile', 'mode')
- probe_grad: float32 [2, 2, 128, 128], P('mode')
The draws below stay inside these ranges and needn't reach their ends.
All inputs are finite; a program needn't handle non-finite values.
Results may differ from the reference program's by a relative error of at most 0.0024.
The reference program's roundings to bfloat16 on the way count: a program that leaves them out, or rounds other values in their place, can miss the bound.
Values sent between devices are 32-bit elements; how exact they have to be, the bound alone decides.
A program may use at most 64 MiB of HBM per device.

```python
import math
import jax
import jax.numpy as jnp
from jax import lax

PATCH = 128
HALO = 64
MODES = 2
STRIP = 128
COLS = 1024
POS_DEV = 16
ROWS = 2048
POSITIONS = 256
N_TILE = 16


def place_ends(values, rng, low, top_value):
    index_at = [jax.random.randint(jax.random.fold_in(rng, axis), (), 0, length) for axis, length in enumerate(values.shape)]
    main_axis = values.shape.index(max(values.shape))
    next_to = index_at[:main_axis] + [(index_at[main_axis] + 1) % values.shape[main_axis]] + index_at[main_axis + 1:]
    return values.at[tuple(index_at)].set(low).at[tuple(next_to)].set(top_value)


def block_levels(own_key, extent, shards, least, high):
    def one(dim, blocks):
        steps = jax.random.uniform(jax.random.fold_in(jax.random.fold_in(own_key, 6), dim), (blocks,), jnp.float32, least / len(shards), high / len(shards))
        return jnp.repeat(jnp.exp(steps), extent[dim] // blocks).reshape((-1,) + (1,) * (len(extent) - dim - 1))

    level = one(*shards[0])
    for cut in shards[1:]:
        level = level * one(*cut)
    return level


def scatter_about(own_key, shape, deviation, reach, cuts=(), held_as=jnp.bfloat16):
    array = deviation * jax.random.normal(own_key, shape, jnp.float32)
    if cuts:
        array = array * block_levels(own_key, shape, cuts, -0.22, 0.18)
    return jnp.clip(array, -reach, reach).astype(held_as)


def setup_inputs(seed: int = 0) -> dict:
    splits = jax.random.split(jax.random.key(seed), 6)
    return {
        "object_wave": scatter_about(splits[0], (2, ROWS, COLS), 1.0, 6.0, ((1, 16),), jnp.float32),
        "probe": scatter_about(splits[1], (MODES, 2, PATCH, PATCH), (4 * MODES) ** -0.5, 2.0, ((0, 2),), jnp.float32),
        "amplitudes": jnp.clip(jnp.exp(math.log(2.5) - 2.3025851 * jax.random.uniform(splits[2], (POSITIONS, PATCH, PATCH), jnp.float32) ** block_levels(splits[2], (POSITIONS, PATCH, PATCH), ((0, 16),), -0.2, 0.2)), 0.25, 2.5).astype(jnp.bfloat16),
        "row_offsets": place_ends(jax.random.randint(splits[3], (POSITIONS,), 0, STRIP + 1), jax.random.fold_in(splits[3], 1), 0, STRIP).astype(jnp.int32),
        "column_offsets": place_ends(jax.random.randint(splits[4], (POSITIONS,), 0, COLS - PATCH + 1), jax.random.fold_in(splits[4], 1), 0, COLS - PATCH).astype(jnp.int32),
    }


FLOOR = 0.25

def tables(length):
    index = jnp.arange(length, dtype=jnp.int32)
    phase = index[:, None] * index[None, :] % length
    angle = phase.astype(jnp.float32) * (2.0 * jnp.pi / length)
    scale = 1.0 / jnp.sqrt(jnp.float32(length))
    return ((jnp.cos(angle) * scale).astype(jnp.bfloat16), (jnp.sin(angle) * scale).astype(jnp.bfloat16))

def apply_left(matrix, batch):
    return jnp.einsum('ab,nmbc->nmac', matrix.astype(jnp.float32), batch.astype(jnp.float32), precision=lax.Precision.HIGHEST)

def apply_right(batch, matrix):
    return jnp.einsum('nmab,bc->nmac', batch.astype(jnp.float32), matrix.astype(jnp.float32), precision=lax.Precision.HIGHEST)

def transform(real_part, imaginary, sign):
    cosine, sine = tables(real_part.shape[-1])
    first_real = (apply_left(cosine, real_part) + sign * apply_left(sine, imaginary)).astype(jnp.bfloat16)
    first_imag = (apply_left(cosine, imaginary) - sign * apply_left(sine, real_part)).astype(jnp.bfloat16)
    second_real = apply_right(first_real, cosine) + sign * apply_right(first_imag, sine)
    second_imag = apply_right(first_imag, cosine) - sign * apply_right(first_real, sine)
    return (second_real, second_imag)

def extract(padded, rows, columns, length):
    start = jnp.zeros((), jnp.int32)

    def single(row, column):
        return lax.dynamic_slice(padded, (start, row.astype(jnp.int32), column.astype(jnp.int32)), (2, length, length))
    return jax.vmap(single)(rows, columns)

def deposit(canvas, terms, rows, columns):
    length = terms.shape[-1]
    start = jnp.zeros((), jnp.int32)

    def add_one(index, current):
        where = (start, rows[index].astype(jnp.int32), columns[index].astype(jnp.int32))
        block = lax.dynamic_slice(current, where, (2, length, length))
        return lax.dynamic_update_slice(current, block + terms[index], where)
    return lax.fori_loop(0, terms.shape[0], add_one, canvas)

def position_terms(patches, probe, amplitude):
    object_real = patches[:, None, 0]
    object_imag = patches[:, None, 1]
    probe_real = probe[None, :, 0]
    probe_imag = probe[None, :, 1]
    wave_real = (probe_real * object_real - probe_imag * object_imag).astype(jnp.bfloat16)
    wave_imag = (probe_real * object_imag + probe_imag * object_real).astype(jnp.bfloat16)
    spectra_real, spectra_imag = transform(wave_real, wave_imag, 1.0)
    intensity = lax.optimization_barrier(jnp.sum(spectra_real * spectra_real + spectra_imag * spectra_imag, axis=1))
    factor = 1.0 - amplitude.astype(jnp.float32) / jnp.sqrt(jnp.maximum(intensity, FLOOR))
    chi_real = (factor[:, None] * spectra_real).astype(jnp.bfloat16)
    chi_imag = (factor[:, None] * spectra_imag).astype(jnp.bfloat16)
    back_real, back_imag = transform(chi_real, chi_imag, -1.0)
    object_real_term = lax.optimization_barrier(jnp.sum(probe_real * back_real + probe_imag * back_imag, axis=1))
    object_imag_term = lax.optimization_barrier(jnp.sum(probe_real * back_imag - probe_imag * back_real, axis=1))
    probe_real_term = lax.optimization_barrier(jnp.sum(object_real * back_real + object_imag * back_imag, axis=0))
    probe_imag_term = lax.optimization_barrier(jnp.sum(object_real * back_imag - object_imag * back_real, axis=0))
    return (jnp.stack([object_real_term, object_imag_term], axis=1), jnp.stack([probe_real_term, probe_imag_term], axis=1))

def reference(object_wave, probe, amplitudes, row_offsets, column_offsets):
    padded = jnp.pad(object_wave, ((0, 0), (HALO, HALO), (0, 0)))
    strip_starts = (jnp.arange(N_TILE, dtype=jnp.int32) * STRIP)[:, None]
    rows_all = row_offsets.reshape(N_TILE, POS_DEV).astype(jnp.int32) + strip_starts
    columns_all = column_offsets.reshape(N_TILE, POS_DEV).astype(jnp.int32)
    measured = amplitudes.reshape(N_TILE, POS_DEV, PATCH, PATCH)

    def tile_step(carry, inputs):
        canvas, probe_total = carry
        rows, columns, amplitude = inputs
        patches = extract(padded, rows, columns, PATCH)
        object_terms, probe_terms = position_terms(patches, probe, amplitude)
        canvas = deposit(canvas, object_terms, rows, columns)
        return ((canvas, probe_total + probe_terms), None)
    initial = (jnp.zeros(padded.shape, jnp.float32), jnp.zeros(probe.shape, jnp.float32))
    (canvas, probe_grad), _ = lax.scan(tile_step, initial, (rows_all, columns_all, measured))
    return (canvas[:, HALO:HALO + ROWS], probe_grad)
```

```python
import functools
import jax
import jax.numpy as jnp
import numpy as np
from jax import lax
from jax.experimental import pallas as pl
from jax.experimental.pallas import tpu as pltpu
from jax.sharding import PartitionSpec as P

FLOOR = 0.25
LANES = 128
MESH = pl.DeviceIdType.MESH
F32 = jnp.float32
BF16 = jnp.bfloat16


def tables(length):
    index = np.arange(length, dtype=np.int64)
    angle = (index[:, None] * index[None, :] % length) * (2.0 * np.pi / length)
    cosine, sine = np.cos(angle) / np.sqrt(length), np.sin(angle) / np.sqrt(length)
    forward = np.block([[cosine, sine], [-sine, cosine]])
    adjoint = np.block([[cosine, -sine], [sine, cosine]])
    return jnp.asarray(forward, dtype=BF16), jnp.asarray(adjoint, dtype=BF16)


def device(tile, mode):
    return (tile, mode)


def halo_kernel(n_tile, n_mode, object_ref, probe_ref, ext_ref, probes_ref,
                halo_send, halo_recv, pass_send, pass_recv, probe_send, probe_recv, local_sem, own_sem):
    tile, mode = lax.axis_index("tile"), lax.axis_index("mode")
    strip = object_ref.shape[1]
    margin = (ext_ref.shape[2] - strip) // 2
    blocks = ext_ref.shape[1]
    share = blocks // n_mode
    first = mode * share
    has_up, has_down = tile > 0, tile < n_tile - 1
    up, down = lax.max(tile - 1, 0), lax.min(tile + 1, n_tile - 1)
    partners = [lax.rem(mode + k, n_mode) for k in range(1, n_mode)]

    barrier = pltpu.get_barrier_semaphore()
    for partner in partners:
        pl.semaphore_signal(barrier, inc=1, device_id=device(tile, partner), device_id_type=MESH)

    @pl.when(has_up)
    def _():
        pl.semaphore_signal(barrier, inc=1, device_id=device(up, mode), device_id_type=MESH)

    @pl.when(has_down)
    def _():
        pl.semaphore_signal(barrier, inc=1, device_id=device(down, mode), device_id_type=MESH)

    local = []
    for plane in range(2):
        for block in range(blocks):
            copy = pltpu.make_async_copy(
                object_ref.at[plane, :, pl.ds(block * LANES, LANES)],
                ext_ref.at[plane, block, pl.ds(margin, strip), :],
                local_sem.at[plane, block],
            )
            copy.start()
            local.append(copy)
    own = pltpu.make_async_copy(probe_ref.at[0], probes_ref.at[mode], own_sem)
    own.start()
    pl.semaphore_wait(barrier, n_mode - 1 + has_up.astype(jnp.int32) + has_down.astype(jnp.int32))

    sides = [
        (0, has_down, has_up, down, strip - margin, 0),
        (1, has_up, has_down, up, 0, margin + strip),
    ]

    def halo(side, target, source_row, target_row, plane, k):
        block = first + k
        return pltpu.make_async_remote_copy(
            src_ref=object_ref.at[plane, pl.ds(source_row, margin), pl.ds(pl.multiple_of(block * LANES, LANES), LANES)],
            dst_ref=ext_ref.at[plane, block, pl.ds(target_row, margin), :],
            send_sem=halo_send.at[side, plane, k],
            recv_sem=halo_recv.at[side, plane, k],
            device_id=device(target, mode),
            device_id_type=MESH,
        )

    def forward(side, target_row, plane, k, p):
        part = ext_ref.at[plane, first + k, pl.ds(target_row, margin), :]
        return pltpu.make_async_remote_copy(
            src_ref=part,
            dst_ref=part,
            send_sem=pass_send.at[p, side, plane, k],
            recv_sem=pass_recv.at[p, side, plane, k],
            device_id=device(tile, partners[p]),
            device_id_type=MESH,
        )

    def share_probe(p):
        return pltpu.make_async_remote_copy(
            src_ref=probe_ref.at[0],
            dst_ref=probes_ref.at[mode],
            send_sem=probe_send.at[p],
            recv_sem=probe_recv.at[p],
            device_id=device(tile, partners[p]),
            device_id_type=MESH,
        )

    for plane in range(2):
        for k in range(share):
            for side, sends, _, target, source_row, target_row in sides:

                @pl.when(sends)
                def _():
                    halo(side, target, source_row, target_row, plane, k).start()

    for p in range(n_mode - 1):
        share_probe(p).start()

    for side, _, gets, _, _, target_row in sides:

        @pl.when(jnp.logical_not(gets))
        def _():
            ext_ref[:, :, pl.ds(target_row, margin), :] = jnp.zeros((2, blocks, margin, LANES), F32)

    for plane in range(2):
        for k in range(share):
            for side, _, gets, target, source_row, target_row in sides:

                @pl.when(gets)
                def _():
                    halo(side, target, source_row, target_row, plane, k).wait_recv()
                    for p in range(n_mode - 1):
                        forward(side, target_row, plane, k, p).start()

    for copy in local:
        copy.wait()
    own.wait()
    for p in range(n_mode - 1):
        share_probe(p).wait()
    for plane in range(2):
        for k in range(share):
            for side, sends, gets, target, source_row, target_row in sides:

                @pl.when(gets)
                def _():
                    for p in range(n_mode - 1):
                        forward(side, target_row, plane, k, p).wait()

                @pl.when(sends)
                def _():
                    halo(side, target, source_row, target_row, plane, k).wait_send()


def exchange_halo(n_tile, n_mode, object_wave, probe):
    planes, strip, columns = object_wave.shape
    length = probe.shape[-1]
    blocks = columns // LANES
    share = blocks // n_mode
    peers = max(n_mode - 1, 1)
    dma = pltpu.SemaphoreType.DMA
    vmem = pl.BlockSpec(memory_space=pltpu.VMEM)
    anywhere = pl.BlockSpec(memory_space=pl.ANY)
    return pl.pallas_call(
        functools.partial(halo_kernel, n_tile, n_mode),
        out_shape=(
            jax.ShapeDtypeStruct((planes, blocks, strip + length, LANES), F32),
            jax.ShapeDtypeStruct((n_mode, 2, length, length), F32),
        ),
        in_specs=[anywhere, anywhere],
        out_specs=(vmem, vmem),
        scratch_shapes=[
            dma((2, 2, share)), dma((2, 2, share)),
            dma((peers, 2, 2, share)), dma((peers, 2, 2, share)),
            dma((peers,)), dma((peers,)), dma((2, blocks)), dma,
        ],
        compiler_params=pltpu.CompilerParams(
            collective_id=0, has_side_effects=True, vmem_limit_bytes=40 * 2**20
        ),
        name="halo",
    )(object_wave, probe)


def gradient_kernel(n_mode, rows_ref, columns_ref, ext_ref, probes_ref, amplitude_ref, forward_ref, adjoint_ref,
                    canvas_ref, total_ref, spectra_ref):
    length = probes_ref.shape[-1]
    count = amplitude_ref.shape[0] // n_mode
    blocks = ext_ref.shape[1]
    base = lax.axis_index("mode") * count
    canvas_ref[...] = jnp.zeros_like(canvas_ref)
    total_ref[...] = jnp.zeros_like(total_ref)
    lane = lax.broadcasted_iota(jnp.int32, (length, LANES), 1)
    pairs = [tuple(range(m, min(m + 2, n_mode))) for m in range(0, n_mode, 2)]

    def dot(a, b):
        return jnp.dot(a, b, preferred_element_type=F32)

    def halves(x, row_count):
        top = [x[:length, i * length:(i + 1) * length] for i in range(row_count)]
        low = [x[length:, i * length:(i + 1) * length] for i in range(row_count)]
        return jnp.concatenate([jnp.concatenate([a, b], axis=1) for a, b in zip(top, low)], axis=0)

    def step(index):
        row = rows_ref[base + index]
        column = columns_ref[base + index]
        block = lax.min(lax.shift_right_logical(column, 7), blocks - 2)
        shift = column - block * LANES
        back = lax.bitwise_and(LANES - shift, LANES - 1)
        ahead = lax.bitwise_and(shift, LANES - 1)

        def patch(plane):
            near = pltpu.roll(ext_ref[plane, block, pl.ds(row, length), :], back, 1)
            far = pltpu.roll(ext_ref[plane, block + 1, pl.ds(row, length), :], back, 1)
            return jnp.where(lane < LANES - shift, near, far)

        object_real, object_imag = patch(0), patch(1)
        intensity = jnp.zeros((length, length), F32)
        for number, pair in enumerate(pairs):
            reals, imags = [], []
            for m in pair:
                probe_real, probe_imag = probes_ref[m, 0], probes_ref[m, 1]
                reals.append((probe_real * object_real - probe_imag * object_imag).astype(BF16))
                imags.append((probe_real * object_imag + probe_imag * object_real).astype(BF16))
            wave = jnp.concatenate([jnp.concatenate(reals, axis=1), jnp.concatenate(imags, axis=1)], axis=0)
            half = dot(forward_ref[...], wave).astype(BF16)
            spectrum = dot(halves(half, len(pair)), adjoint_ref[...])
            for i in range(len(pair)):
                part = spectrum[i * length:(i + 1) * length]
                intensity += part[:, :length] * part[:, :length] + part[:, length:] * part[:, length:]
            if len(pairs) > 1:
                spectra_ref[number, :len(pair) * length] = spectrum
        amplitude = amplitude_ref[base + index].astype(F32)
        factor = 1.0 - amplitude * lax.rsqrt(jnp.maximum(intensity, FLOOR))
        term_real = jnp.zeros((length, length), F32)
        term_imag = jnp.zeros((length, length), F32)
        for number, pair in enumerate(pairs):
            if len(pairs) > 1:
                spectrum = spectra_ref[number, :len(pair) * length]
            reals, imags = [], []
            for i in range(len(pair)):
                part = spectrum[i * length:(i + 1) * length]
                reals.append((factor * part[:, :length]).astype(BF16))
                imags.append((factor * part[:, length:]).astype(BF16))
            chi = jnp.concatenate([jnp.concatenate(reals, axis=1), jnp.concatenate(imags, axis=1)], axis=0)
            half = dot(adjoint_ref[...], chi).astype(BF16)
            result = dot(halves(half, len(pair)), forward_ref[...])
            for i, m in enumerate(pair):
                real = result[i * length:(i + 1) * length, :length]
                imag = result[i * length:(i + 1) * length, length:]
                probe_real, probe_imag = probes_ref[m, 0], probes_ref[m, 1]
                term_real += probe_real * real + probe_imag * imag
                term_imag += probe_real * imag - probe_imag * real
                total_ref[m, 0] += object_real * real + object_imag * imag
                total_ref[m, 1] += object_real * imag - object_imag * real
        for plane, term in ((0, term_real), (1, term_imag)):
            moved = pltpu.roll(term, ahead, 1)
            canvas_ref[plane, block, pl.ds(row, length), :] += jnp.where(lane >= shift, moved, 0.0)
            canvas_ref[plane, block + 1, pl.ds(row, length), :] += jnp.where(lane < shift, moved, 0.0)

    @pl.loop(0, count)
    def _(index):
        step(index)


def gradients(n_mode, ext, probes, amplitudes, rows, columns):
    length = probes.shape[-1]
    forward, adjoint = tables(length)
    vmem = pl.BlockSpec(memory_space=pltpu.VMEM)
    smem = pl.BlockSpec(memory_space=pltpu.SMEM)
    return pl.pallas_call(
        functools.partial(gradient_kernel, n_mode),
        out_shape=(
            jax.ShapeDtypeStruct(ext.shape, F32),
            jax.ShapeDtypeStruct(probes.shape, F32),
        ),
        in_specs=[smem, smem, vmem, vmem, vmem, vmem, vmem],
        out_specs=(vmem, vmem),
        scratch_shapes=[pltpu.VMEM(((n_mode + 1) // 2, 2 * length, 2 * length), F32)],
        compiler_params=pltpu.CompilerParams(vmem_limit_bytes=40 * 2**20),
        name="gradient",
    )(rows, columns, ext, probes, amplitudes, forward, adjoint)


def sum_kernel(n_tile, n_mode, canvas_ref, partial_ref, object_ref, probe_ref,
               landed, rim_out, rim_in, probe_in, probe_own, chunks_in,
               mode_send, mode_recv, rim_send, rim_recv, part_send, part_recv,
               scatter_send, scatter_recv, gather_send, gather_recv):
    tile, mode = lax.axis_index("tile"), lax.axis_index("mode")
    strip = object_ref.shape[1]
    extent = canvas_ref.shape[2]
    margin = (extent - strip) // 2
    share = landed.shape[2]
    chunk = chunks_in.shape[1]
    reducers = probe_own.shape[0] // chunk
    has_up, has_down = tile > 0, tile < n_tile - 1
    up, down = lax.max(tile - 1, 0), lax.min(tile + 1, n_tile - 1)
    partners = [lax.rem(mode + k, n_mode) for k in range(1, n_mode)]

    barrier = pltpu.get_barrier_semaphore()
    for partner in partners:
        pl.semaphore_signal(barrier, inc=1, device_id=device(tile, partner), device_id_type=MESH)

    @pl.loop(1, n_tile)
    def _(k):
        pl.semaphore_signal(barrier, inc=1, device_id=device(lax.rem(tile + k, n_tile), mode), device_id_type=MESH)

    pl.semaphore_wait(barrier, n_mode - 1 + n_tile - 1)

    sections = [(0, margin), (margin + strip, margin), (margin, strip)]

    def to_mode(p, section, plane):
        start, size = sections[section]
        return pltpu.make_async_remote_copy(
            src_ref=canvas_ref.at[plane, pl.ds(partners[p] * share, share), pl.ds(start, size), :],
            dst_ref=landed.at[p, plane, :, pl.ds(start, size), :],
            send_sem=mode_send.at[p, section, plane],
            recv_sem=mode_recv.at[p, section, plane],
            device_id=device(tile, partners[p]),
            device_id_type=MESH,
        )

    def part_to_mode(p):
        return pltpu.make_async_remote_copy(
            src_ref=partial_ref.at[partners[p]],
            dst_ref=probe_in.at[p],
            send_sem=part_send.at[p],
            recv_sem=part_recv.at[p],
            device_id=device(tile, partners[p]),
            device_id_type=MESH,
        )

    def rim(side, plane):
        return pltpu.make_async_remote_copy(
            src_ref=rim_out.at[side, plane],
            dst_ref=rim_in.at[side, plane],
            send_sem=rim_send.at[side, plane],
            recv_sem=rim_recv.at[side, plane],
            device_id=device(up if side == 0 else down, mode),
            device_id_type=MESH,
        )

    for p in range(n_mode - 1):
        part_to_mode(p).start()
    for section in (0, 1, 2):
        for plane in range(2):
            for p in range(n_mode - 1):
                to_mode(p, section, plane).start()

    own_part = partial_ref[mode]
    for p in range(n_mode - 1):
        part_to_mode(p).wait_recv()
        own_part += probe_in[p]
    probe_own[...] = own_part.reshape(probe_own.shape)

    def scatter(k):
        target = lax.rem(tile + k, n_tile)
        return target, pltpu.make_async_remote_copy(
            src_ref=probe_own.at[pl.ds(pl.multiple_of(lax.rem(target, reducers) * chunk, chunk), chunk), :],
            dst_ref=chunks_in.at[k - 1],
            send_sem=scatter_send.at[k - 1],
            recv_sem=scatter_recv.at[k - 1],
            device_id=device(target, mode),
            device_id_type=MESH,
        )

    @pl.loop(1, n_tile)
    def _(k):
        target, copy = scatter(k)

        @pl.when(target < reducers)
        def _():
            copy.start()

    mine = pl.ds(mode * share, share)
    for section, sends in ((0, has_up), (1, has_down)):
        start, size = sections[section]
        for plane in range(2):
            value = canvas_ref[plane, mine, start:start + size, :]
            for p in range(n_mode - 1):
                to_mode(p, section, plane).wait_recv()
                value += landed[p, plane, :, start:start + size, :]
            rim_out[section, plane] = value

            @pl.when(sends)
            def _():
                rim(section, plane).start()

    rows_mine = pl.ds(pl.multiple_of(lax.rem(tile, reducers) * chunk, chunk), chunk)

    def gather(k):
        target = lax.rem(tile + k, n_tile)
        return pltpu.make_async_remote_copy(
            src_ref=probe_ref.at[rows_mine, :],
            dst_ref=probe_ref.at[rows_mine, :],
            send_sem=gather_send.at[k - 1],
            recv_sem=gather_recv.at[k - 1],
            device_id=device(target, mode),
            device_id_type=MESH,
        )

    def source(k):
        return lax.rem(tile + n_tile - k, n_tile)

    @pl.when(tile < reducers)
    def _():
        @pl.loop(1, n_tile)
        def _(k):
            scatter(k)[1].wait_recv()

        value = probe_own[rows_mine, :]
        for k in range(n_tile - 1):
            value += chunks_in[k]
        probe_ref[rows_mine, :] = value

        @pl.loop(1, n_tile)
        def _(k):
            gather(k).start()

    start, size = sections[2]
    for plane in range(2):
        value = canvas_ref[plane, mine, start:start + size, :]
        for p in range(n_mode - 1):
            to_mode(p, 2, plane).wait_recv()
            value += landed[p, plane, :, start:start + size, :]
        for k in range(share):
            object_ref[plane, :, k * LANES:(k + 1) * LANES] = value[k]
    for side, gets, row in ((0, has_down, strip - margin), (1, has_up, 0)):
        for plane in range(2):

            @pl.when(gets)
            def _():
                rim(side, plane).wait_recv()
                for k in range(share):
                    object_ref[plane, row:row + margin, k * LANES:(k + 1) * LANES] += rim_in[side, plane, k]

    @pl.loop(1, n_tile)
    def _(k):
        @pl.when(source(k) < reducers)
        def _():
            gather(k).wait_recv()

        target, copy = scatter(k)

        @pl.when(target < reducers)
        def _():
            copy.wait_send()

        @pl.when(tile < reducers)
        def _():
            gather(k).wait_send()

    for p in range(n_mode - 1):
        part_to_mode(p).wait_send()
        for section in range(3):
            for plane in range(2):
                to_mode(p, section, plane).wait_send()
    for section, sends in ((0, has_up), (1, has_down)):

        @pl.when(sends)
        def _():
            for plane in range(2):
                rim(section, plane).wait_send()


def sum_gradients(n_tile, n_mode, canvas, partial, margin):
    planes, blocks, extent, _ = canvas.shape
    length = partial.shape[-1]
    share = blocks // n_mode
    strip = extent - 2 * margin
    peers = max(n_mode - 1, 1)
    chunk = max(2 * length // n_tile, 8)
    dma = pltpu.SemaphoreType.DMA
    vmem = pl.BlockSpec(memory_space=pltpu.VMEM)
    others = n_tile - 1
    object_grad, probe_grad = pl.pallas_call(
        functools.partial(sum_kernel, n_tile, n_mode),
        out_shape=(
            jax.ShapeDtypeStruct((planes, strip, share * LANES), F32),
            jax.ShapeDtypeStruct((2 * length, length), F32),
        ),
        in_specs=[vmem, vmem],
        out_specs=(vmem, vmem),
        scratch_shapes=[
            pltpu.VMEM((peers, planes, share, extent, LANES), F32),
            pltpu.VMEM((2, planes, share, margin, LANES), F32),
            pltpu.VMEM((2, planes, share, margin, LANES), F32),
            pltpu.VMEM((peers, 2, length, length), F32),
            pltpu.VMEM((2 * length, length), F32),
            pltpu.VMEM((others, chunk, length), F32),
            dma((peers, 3, planes)), dma((peers, 3, planes)),
            dma((2, planes)), dma((2, planes)),
            dma((peers,)), dma((peers,)),
            dma((others,)), dma((others,)), dma((others,)), dma((others,)),
        ],
        compiler_params=pltpu.CompilerParams(
            collective_id=1, has_side_effects=True, vmem_limit_bytes=40 * 2**20
        ),
        name="sums",
    )(canvas, partial)
    return object_grad, probe_grad.reshape(1, 2, length, length)


def solution(mesh):
    n_tile, n_mode = mesh.shape["tile"], mesh.shape["mode"]

    def body(object_wave, probe, amplitudes, rows, columns):
        ext, probes = exchange_halo(n_tile, n_mode, object_wave, probe)
        canvas, partial = gradients(n_mode, ext, probes, amplitudes, rows, columns)
        return sum_gradients(n_tile, n_mode, canvas, partial, probe.shape[-1] // 2)

    placed = (
        P(None, "tile", None),
        P("mode", None, None, None),
        P("tile", None, None),
        P("tile"),
        P("tile"),
    )
    return jax.shard_map(
        body,
        mesh=mesh,
        in_specs=placed,
        out_specs=(P(None, "tile", "mode"), P("mode", None, None, None)),
        check_vma=False,
    )
```

```python
import functools
import jax
import jax.numpy as jnp
import numpy as np
from jax import lax
from jax.experimental import pallas as pl
from jax.experimental.pallas import tpu as pltpu
from jax.sharding import PartitionSpec as P

FLOOR = 0.25
LANES = 128
MESH = pl.DeviceIdType.MESH
F32 = jnp.float32
BF16 = jnp.bfloat16


def tables(length):
    index = np.arange(length, dtype=np.int64)
    angle = (index[:, None] * index[None, :] % length) * (2.0 * np.pi / length)
    cosine, sine = np.cos(angle) / np.sqrt(length), np.sin(angle) / np.sqrt(length)
    forward = np.block([[cosine, sine], [-sine, cosine]])
    adjoint = np.block([[cosine, -sine], [sine, cosine]])
    return jnp.asarray(np.stack([forward, adjoint]), dtype=BF16)


def device(tile, mode):
    return (tile, mode)


def halo_kernel(n_tile, n_mode, object_ref, probe_ref, amplitude_ref, rows_ref, columns_ref, table_ref,
                ext_ref, probes_ref, amplitude_out, rows_out, columns_out, table_out,
                halo_send, halo_recv, pass_send, pass_recv, probe_send, probe_recv, local_sem, own_sem):
    tile, mode = lax.axis_index("tile"), lax.axis_index("mode")
    strip = object_ref.shape[1]
    margin = (ext_ref.shape[2] - strip) // 2
    blocks = ext_ref.shape[1]
    share = blocks // n_mode
    first = mode * share
    has_up, has_down = tile > 0, tile < n_tile - 1
    up, down = lax.max(tile - 1, 0), lax.min(tile + 1, n_tile - 1)
    partners = [lax.rem(mode + k, n_mode) for k in range(1, n_mode)]

    barrier = pltpu.get_barrier_semaphore()
    for partner in partners:
        pl.semaphore_signal(barrier, inc=1, device_id=device(tile, partner), device_id_type=MESH)

    @pl.when(has_up)
    def _():
        pl.semaphore_signal(barrier, inc=1, device_id=device(up, mode), device_id_type=MESH)

    @pl.when(has_down)
    def _():
        pl.semaphore_signal(barrier, inc=1, device_id=device(down, mode), device_id_type=MESH)

    local = []
    for plane in range(2):
        for block in range(blocks):
            copy = pltpu.make_async_copy(
                object_ref.at[plane, :, pl.ds(block * LANES, LANES)],
                ext_ref.at[plane, block, pl.ds(margin, strip), :],
                local_sem.at[plane, block],
            )
            copy.start()
            local.append(copy)
    count = amplitude_out.shape[0]
    held = [
        (probe_ref.at[0], probes_ref.at[mode]),
        (amplitude_ref.at[pl.ds(mode * count, count)], amplitude_out),
        (rows_ref, rows_out),
        (columns_ref, columns_out),
        (table_ref, table_out),
    ]
    for number, (source, target) in enumerate(held):
        copy = pltpu.make_async_copy(source, target, own_sem.at[number])
        copy.start()
        local.append(copy)
    pl.semaphore_wait(barrier, n_mode - 1 + has_up.astype(jnp.int32) + has_down.astype(jnp.int32))

    sides = [
        (0, has_down, has_up, down, strip - margin, 0),
        (1, has_up, has_down, up, 0, margin + strip),
    ]

    def halo(side, target, source_row, target_row, plane, k):
        block = first + k
        return pltpu.make_async_remote_copy(
            src_ref=object_ref.at[plane, pl.ds(source_row, margin), pl.ds(pl.multiple_of(block * LANES, LANES), LANES)],
            dst_ref=ext_ref.at[plane, block, pl.ds(target_row, margin), :],
            send_sem=halo_send.at[side, plane, k],
            recv_sem=halo_recv.at[side, plane, k],
            device_id=device(target, mode),
            device_id_type=MESH,
        )

    def forward(side, target_row, plane, k, p):
        part = ext_ref.at[plane, first + k, pl.ds(target_row, margin), :]
        return pltpu.make_async_remote_copy(
            src_ref=part,
            dst_ref=part,
            send_sem=pass_send.at[p, side, plane, k],
            recv_sem=pass_recv.at[p, side, plane, k],
            device_id=device(tile, partners[p]),
            device_id_type=MESH,
        )

    def share_probe(p):
        return pltpu.make_async_remote_copy(
            src_ref=probe_ref.at[0],
            dst_ref=probes_ref.at[mode],
            send_sem=probe_send.at[p],
            recv_sem=probe_recv.at[p],
            device_id=device(tile, partners[p]),
            device_id_type=MESH,
        )

    for plane in range(2):
        for k in range(share):
            for side, sends, _, target, source_row, target_row in sides:

                @pl.when(sends)
                def _():
                    halo(side, target, source_row, target_row, plane, k).start()

    for p in range(n_mode - 1):
        share_probe(p).start()

    for side, _, gets, _, _, target_row in sides:

        @pl.when(jnp.logical_not(gets))
        def _():
            ext_ref[:, :, pl.ds(target_row, margin), :] = jnp.zeros((2, blocks, margin, LANES), F32)

    for plane in range(2):
        for k in range(share):
            for side, _, gets, target, source_row, target_row in sides:

                @pl.when(gets)
                def _():
                    halo(side, target, source_row, target_row, plane, k).wait_recv()
                    for p in range(n_mode - 1):
                        forward(side, target_row, plane, k, p).start()

    for copy in local:
        copy.wait()
    for p in range(n_mode - 1):
        share_probe(p).wait()
    for plane in range(2):
        for k in range(share):
            for side, sends, gets, target, source_row, target_row in sides:

                @pl.when(gets)
                def _():
                    for p in range(n_mode - 1):
                        forward(side, target_row, plane, k, p).wait()

                @pl.when(sends)
                def _():
                    halo(side, target, source_row, target_row, plane, k).wait_send()


def exchange_halo(n_tile, n_mode, object_wave, probe, amplitudes, rows, columns_at):
    planes, strip, columns = object_wave.shape
    length = probe.shape[-1]
    blocks = columns // LANES
    share = blocks // n_mode
    peers = max(n_mode - 1, 1)
    dma = pltpu.SemaphoreType.DMA
    vmem = pl.BlockSpec(memory_space=pltpu.VMEM)
    hbm = pl.BlockSpec(memory_space=pltpu.HBM)
    table = tables(length)
    count = amplitudes.shape[0] // n_mode
    return pl.pallas_call(
        functools.partial(halo_kernel, n_tile, n_mode),
        out_shape=(
            jax.ShapeDtypeStruct((planes, blocks, strip + length, LANES), F32),
            jax.ShapeDtypeStruct((n_mode, 2, length, length), F32),
            jax.ShapeDtypeStruct((count,) + amplitudes.shape[1:], amplitudes.dtype),
            jax.ShapeDtypeStruct(rows.shape, rows.dtype),
            jax.ShapeDtypeStruct(columns_at.shape, columns_at.dtype),
            jax.ShapeDtypeStruct(table.shape, table.dtype),
        ),
        in_specs=[hbm] * 6,
        out_specs=(vmem,) * 6,
        scratch_shapes=[
            dma((2, 2, share)), dma((2, 2, share)),
            dma((peers, 2, 2, share)), dma((peers, 2, 2, share)),
            dma((peers,)), dma((peers,)), dma((2, blocks)), dma((5,)),
        ],
        compiler_params=pltpu.CompilerParams(
            collective_id=0, has_side_effects=True, vmem_limit_bytes=40 * 2**20
        ),
        name="halo",
    )(*[pltpu.with_memory_space_constraint(x, pltpu.HBM)
        for x in (object_wave, probe, amplitudes, rows, columns_at, table)])


def gradient_kernel(n_mode, rows_ref, columns_ref, ext_ref, probes_ref, amplitude_ref, table_ref,
                    canvas_ref, total_ref, spectra_ref):
    length = probes_ref.shape[-1]
    count = amplitude_ref.shape[0]
    forward_ref, adjoint_ref = table_ref.at[0], table_ref.at[1]
    blocks = ext_ref.shape[1]
    base = lax.axis_index("mode") * count
    canvas_ref[...] = jnp.zeros_like(canvas_ref)
    total_ref[...] = jnp.zeros_like(total_ref)
    lane = lax.broadcasted_iota(jnp.int32, (length, LANES), 1)
    pairs = [tuple(range(m, min(m + 2, n_mode))) for m in range(0, n_mode, 2)]

    def dot(a, b):
        return jnp.dot(a, b, preferred_element_type=F32)

    def halves(x, row_count):
        top = [x[:length, i * length:(i + 1) * length] for i in range(row_count)]
        low = [x[length:, i * length:(i + 1) * length] for i in range(row_count)]
        return jnp.concatenate([jnp.concatenate([a, b], axis=1) for a, b in zip(top, low)], axis=0)

    def step(index):
        row = rows_ref[base + index]
        column = columns_ref[base + index]
        block = lax.min(lax.shift_right_logical(column, 7), blocks - 2)
        shift = column - block * LANES
        back = lax.bitwise_and(LANES - shift, LANES - 1)
        ahead = lax.bitwise_and(shift, LANES - 1)

        def patch(plane):
            near = pltpu.roll(ext_ref[plane, block, pl.ds(row, length), :], back, 1)
            far = pltpu.roll(ext_ref[plane, block + 1, pl.ds(row, length), :], back, 1)
            return jnp.where(lane < LANES - shift, near, far)

        object_real, object_imag = patch(0), patch(1)
        intensity = jnp.zeros((length, length), F32)
        for number, pair in enumerate(pairs):
            reals, imags = [], []
            for m in pair:
                probe_real, probe_imag = probes_ref[m, 0], probes_ref[m, 1]
                reals.append((probe_real * object_real - probe_imag * object_imag).astype(BF16))
                imags.append((probe_real * object_imag + probe_imag * object_real).astype(BF16))
            wave = jnp.concatenate([jnp.concatenate(reals, axis=1), jnp.concatenate(imags, axis=1)], axis=0)
            half = dot(forward_ref[...], wave).astype(BF16)
            spectrum = dot(halves(half, len(pair)), adjoint_ref[...])
            for i in range(len(pair)):
                part = spectrum[i * length:(i + 1) * length]
                intensity += part[:, :length] * part[:, :length] + part[:, length:] * part[:, length:]
            if len(pairs) > 1:
                spectra_ref[number, :len(pair) * length] = spectrum
        amplitude = amplitude_ref[index].astype(F32)
        factor = 1.0 - amplitude * lax.rsqrt(jnp.maximum(intensity, FLOOR))
        term_real = jnp.zeros((length, length), F32)
        term_imag = jnp.zeros((length, length), F32)
        for number, pair in enumerate(pairs):
            if len(pairs) > 1:
                spectrum = spectra_ref[number, :len(pair) * length]
            reals, imags = [], []
            for i in range(len(pair)):
                part = spectrum[i * length:(i + 1) * length]
                reals.append((factor * part[:, :length]).astype(BF16))
                imags.append((factor * part[:, length:]).astype(BF16))
            chi = jnp.concatenate([jnp.concatenate(reals, axis=1), jnp.concatenate(imags, axis=1)], axis=0)
            half = dot(adjoint_ref[...], chi).astype(BF16)
            result = dot(halves(half, len(pair)), forward_ref[...])
            for i, m in enumerate(pair):
                real = result[i * length:(i + 1) * length, :length]
                imag = result[i * length:(i + 1) * length, length:]
                probe_real, probe_imag = probes_ref[m, 0], probes_ref[m, 1]
                term_real += probe_real * real + probe_imag * imag
                term_imag += probe_real * imag - probe_imag * real
                total_ref[m, 0] += object_real * real + object_imag * imag
                total_ref[m, 1] += object_real * imag - object_imag * real
        for plane, term in ((0, term_real), (1, term_imag)):
            moved = pltpu.roll(term, ahead, 1)
            canvas_ref[plane, block, pl.ds(row, length), :] += jnp.where(lane >= shift, moved, 0.0)
            canvas_ref[plane, block + 1, pl.ds(row, length), :] += jnp.where(lane < shift, moved, 0.0)

    @pl.loop(0, count, unroll=2)
    def _(index):
        step(index)


def gradients(n_mode, ext, probes, amplitudes, rows, columns, table):
    length = probes.shape[-1]
    vmem = pl.BlockSpec(memory_space=pltpu.VMEM)
    smem = pl.BlockSpec(memory_space=pltpu.SMEM)
    return pl.pallas_call(
        functools.partial(gradient_kernel, n_mode),
        out_shape=(
            jax.ShapeDtypeStruct(ext.shape, F32),
            jax.ShapeDtypeStruct(probes.shape, F32),
        ),
        in_specs=[smem, smem, vmem, vmem, vmem, vmem],
        out_specs=(vmem, vmem),
        scratch_shapes=[pltpu.VMEM(((n_mode + 1) // 2, 2 * length, 2 * length), F32)],
        compiler_params=pltpu.CompilerParams(vmem_limit_bytes=40 * 2**20),
        name="gradient",
    )(rows, columns, ext, probes, amplitudes, table)


def sum_kernel(n_tile, n_mode, canvas_ref, partial_ref, object_ref, probe_ref,
               landed, rim_out, rim_in, probe_in, probe_own, chunks_in,
               mode_send, mode_recv, rim_send, rim_recv, part_send, part_recv,
               scatter_send, scatter_recv, gather_send, gather_recv):
    tile, mode = lax.axis_index("tile"), lax.axis_index("mode")
    strip = object_ref.shape[1]
    extent = canvas_ref.shape[2]
    margin = (extent - strip) // 2
    share = landed.shape[2]
    chunk = chunks_in.shape[1]
    reducers = probe_own.shape[0] // chunk
    has_up, has_down = tile > 0, tile < n_tile - 1
    up, down = lax.max(tile - 1, 0), lax.min(tile + 1, n_tile - 1)
    partners = [lax.rem(mode + k, n_mode) for k in range(1, n_mode)]

    barrier = pltpu.get_barrier_semaphore()
    for partner in partners:
        pl.semaphore_signal(barrier, inc=1, device_id=device(tile, partner), device_id_type=MESH)

    @pl.loop(1, n_tile)
    def _(k):
        pl.semaphore_signal(barrier, inc=1, device_id=device(lax.rem(tile + k, n_tile), mode), device_id_type=MESH)

    pl.semaphore_wait(barrier, n_mode - 1 + n_tile - 1)

    sections = [(0, margin), (margin + strip, margin), (margin, strip)]

    def to_mode(p, section, plane):
        start, size = sections[section]
        return pltpu.make_async_remote_copy(
            src_ref=canvas_ref.at[plane, pl.ds(partners[p] * share, share), pl.ds(start, size), :],
            dst_ref=landed.at[p, plane, :, pl.ds(start, size), :],
            send_sem=mode_send.at[p, section, plane],
            recv_sem=mode_recv.at[p, section, plane],
            device_id=device(tile, partners[p]),
            device_id_type=MESH,
        )

    def part_to_mode(p):
        return pltpu.make_async_remote_copy(
            src_ref=partial_ref.at[partners[p]],
            dst_ref=probe_in.at[p],
            send_sem=part_send.at[p],
            recv_sem=part_recv.at[p],
            device_id=device(tile, partners[p]),
            device_id_type=MESH,
        )

    def rim(side, plane):
        return pltpu.make_async_remote_copy(
            src_ref=rim_out.at[side, plane],
            dst_ref=rim_in.at[side, plane],
            send_sem=rim_send.at[side, plane],
            recv_sem=rim_recv.at[side, plane],
            device_id=device(up if side == 0 else down, mode),
            device_id_type=MESH,
        )

    for p in range(n_mode - 1):
        part_to_mode(p).start()
    for section in (0, 1, 2):
        for plane in range(2):
            for p in range(n_mode - 1):
                to_mode(p, section, plane).start()

    own_part = partial_ref[mode]
    for p in range(n_mode - 1):
        part_to_mode(p).wait_recv()
        own_part += probe_in[p]
    probe_own[...] = own_part.reshape(probe_own.shape)

    def scatter(k):
        target = lax.rem(tile + k, n_tile)
        return target, pltpu.make_async_remote_copy(
            src_ref=probe_own.at[pl.ds(pl.multiple_of(lax.rem(target, reducers) * chunk, chunk), chunk), :],
            dst_ref=chunks_in.at[k - 1],
            send_sem=scatter_send.at[k - 1],
            recv_sem=scatter_recv.at[k - 1],
            device_id=device(target, mode),
            device_id_type=MESH,
        )

    @pl.loop(1, n_tile)
    def _(k):
        target, copy = scatter(k)

        @pl.when(target < reducers)
        def _():
            copy.start()

    mine = pl.ds(mode * share, share)
    for section, sends in ((0, has_up), (1, has_down)):
        start, size = sections[section]
        for plane in range(2):
            value = canvas_ref[plane, mine, start:start + size, :]
            for p in range(n_mode - 1):
                to_mode(p, section, plane).wait_recv()
                value += landed[p, plane, :, start:start + size, :]
            rim_out[section, plane] = value

            @pl.when(sends)
            def _():
                rim(section, plane).start()

    rows_mine = pl.ds(pl.multiple_of(lax.rem(tile, reducers) * chunk, chunk), chunk)

    def gather(k):
        target = lax.rem(tile + k, n_tile)
        return pltpu.make_async_remote_copy(
            src_ref=probe_ref.at[rows_mine, :],
            dst_ref=probe_ref.at[rows_mine, :],
            send_sem=gather_send.at[k - 1],
            recv_sem=gather_recv.at[k - 1],
            device_id=device(target, mode),
            device_id_type=MESH,
        )

    def source(k):
        return lax.rem(tile + n_tile - k, n_tile)

    @pl.when(tile < reducers)
    def _():
        @pl.loop(1, n_tile)
        def _(k):
            scatter(k)[1].wait_recv()

        value = probe_own[rows_mine, :]
        for k in range(n_tile - 1):
            value += chunks_in[k]
        probe_ref[rows_mine, :] = value

        @pl.loop(1, n_tile)
        def _(k):
            gather(k).start()

    start, size = sections[2]
    for plane in range(2):
        value = canvas_ref[plane, mine, start:start + size, :]
        for p in range(n_mode - 1):
            to_mode(p, 2, plane).wait_recv()
            value += landed[p, plane, :, start:start + size, :]
        for k in range(share):
            object_ref[plane, :, k * LANES:(k + 1) * LANES] = value[k]
    for side, gets, row in ((0, has_down, strip - margin), (1, has_up, 0)):
        for plane in range(2):

            @pl.when(gets)
            def _():
                rim(side, plane).wait_recv()
                for k in range(share):
                    object_ref[plane, row:row + margin, k * LANES:(k + 1) * LANES] += rim_in[side, plane, k]

    @pl.loop(1, n_tile)
    def _(k):
        @pl.when(source(k) < reducers)
        def _():
            gather(k).wait_recv()

        target, copy = scatter(k)

        @pl.when(target < reducers)
        def _():
            copy.wait_send()

        @pl.when(tile < reducers)
        def _():
            gather(k).wait_send()

    for p in range(n_mode - 1):
        part_to_mode(p).wait_send()
        for section in range(3):
            for plane in range(2):
                to_mode(p, section, plane).wait_send()
    for section, sends in ((0, has_up), (1, has_down)):

        @pl.when(sends)
        def _():
            for plane in range(2):
                rim(section, plane).wait_send()


def sum_gradients(n_tile, n_mode, canvas, partial, margin):
    planes, blocks, extent, _ = canvas.shape
    length = partial.shape[-1]
    share = blocks // n_mode
    strip = extent - 2 * margin
    peers = max(n_mode - 1, 1)
    chunk = max(2 * length // n_tile, 8)
    dma = pltpu.SemaphoreType.DMA
    vmem = pl.BlockSpec(memory_space=pltpu.VMEM)
    others = n_tile - 1
    object_grad, probe_grad = pl.pallas_call(
        functools.partial(sum_kernel, n_tile, n_mode),
        out_shape=(
            jax.ShapeDtypeStruct((planes, strip, share * LANES), F32),
            jax.ShapeDtypeStruct((2 * length, length), F32),
        ),
        in_specs=[vmem, vmem],
        out_specs=(vmem, vmem),
        scratch_shapes=[
            pltpu.VMEM((peers, planes, share, extent, LANES), F32),
            pltpu.VMEM((2, planes, share, margin, LANES), F32),
            pltpu.VMEM((2, planes, share, margin, LANES), F32),
            pltpu.VMEM((peers, 2, length, length), F32),
            pltpu.VMEM((2 * length, length), F32),
            pltpu.VMEM((others, chunk, length), F32),
            dma((peers, 3, planes)), dma((peers, 3, planes)),
            dma((2, planes)), dma((2, planes)),
            dma((peers,)), dma((peers,)),
            dma((others,)), dma((others,)), dma((others,)), dma((others,)),
        ],
        compiler_params=pltpu.CompilerParams(
            collective_id=1, has_side_effects=True, vmem_limit_bytes=40 * 2**20
        ),
        name="sums",
    )(canvas, partial)
    return object_grad, probe_grad.reshape(1, 2, length, length)


def solution(mesh):
    n_tile, n_mode = mesh.shape["tile"], mesh.shape["mode"]

    def body(object_wave, probe, amplitudes, rows, columns):
        held = exchange_halo(n_tile, n_mode, object_wave, probe, amplitudes, rows, columns)
        canvas, partial = gradients(n_mode, *held)
        return sum_gradients(n_tile, n_mode, canvas, partial, probe.shape[-1] // 2)

    placed = (
        P(None, "tile", None),
        P("mode", None, None, None),
        P("tile", None, None),
        P("tile"),
        P("tile"),
    )
    return jax.shard_map(
        body,
        mesh=mesh,
        in_specs=placed,
        out_specs=(P(None, "tile", "mode"), P("mode", None, None, None)),
        check_vma=False,
    )
```

```python
import functools
import jax
import jax.numpy as jnp
import numpy as np
from jax import lax
from jax.experimental import pallas as pl
from jax.experimental.pallas import tpu as pltpu
from jax.sharding import PartitionSpec as P

FLOOR = 0.25
LANES = 128
WINDOW = 8
MESH = pl.DeviceIdType.MESH
F32 = jnp.float32
BF16 = jnp.bfloat16


def tables(length):
    index = np.arange(length, dtype=np.int64)
    angle = (index[:, None] * index[None, :] % length) * (2.0 * np.pi / length)
    cosine, sine = np.cos(angle) / np.sqrt(length), np.sin(angle) / np.sqrt(length)
    forward = np.block([[cosine, sine], [-sine, cosine]])
    adjoint = np.block([[cosine, -sine], [sine, cosine]])
    return jnp.asarray(np.stack([forward, adjoint]), dtype=BF16)


def device(tile, mode):
    return (tile, mode)


def halo_kernel(n_tile, n_mode, object_ref, probe_ref, amplitude_ref, rows_ref, columns_ref, table_ref,
                ext_ref, probes_ref, amplitude_out, rows_out, columns_out, table_out,
                halo_send, halo_recv, pass_send, pass_recv, probe_send, probe_recv, local_sem, own_sem):
    tile, mode = lax.axis_index("tile"), lax.axis_index("mode")
    strip = object_ref.shape[1]
    margin = (ext_ref.shape[2] - strip) // 2
    blocks = ext_ref.shape[1]
    share = blocks // n_mode
    first = mode * share
    has_up, has_down = tile > 0, tile < n_tile - 1
    up, down = lax.max(tile - 1, 0), lax.min(tile + 1, n_tile - 1)
    partners = [lax.rem(mode + k, n_mode) for k in range(1, n_mode)]

    barrier = pltpu.get_barrier_semaphore()
    for partner in partners:
        pl.semaphore_signal(barrier, inc=1, device_id=device(tile, partner), device_id_type=MESH)

    @pl.when(has_up)
    def _():
        pl.semaphore_signal(barrier, inc=1, device_id=device(up, mode), device_id_type=MESH)

    @pl.when(has_down)
    def _():
        pl.semaphore_signal(barrier, inc=1, device_id=device(down, mode), device_id_type=MESH)

    local = []
    for plane in range(2):
        for block in range(blocks):
            copy = pltpu.make_async_copy(
                object_ref.at[plane, :, pl.ds(block * LANES, LANES)],
                ext_ref.at[plane, block, pl.ds(margin, strip), :],
                local_sem.at[plane, block],
            )
            copy.start()
            local.append(copy)
    count = amplitude_out.shape[0]
    held = [
        (probe_ref.at[0], probes_ref.at[mode]),
        (amplitude_ref.at[pl.ds(mode * count, count)], amplitude_out),
        (rows_ref, rows_out),
        (columns_ref, columns_out),
        (table_ref, table_out),
    ]
    for number, (source, target) in enumerate(held):
        copy = pltpu.make_async_copy(source, target, own_sem.at[number])
        copy.start()
        local.append(copy)
    pl.semaphore_wait(barrier, n_mode - 1 + has_up.astype(jnp.int32) + has_down.astype(jnp.int32))

    sides = [
        (0, has_down, has_up, down, strip - margin, 0),
        (1, has_up, has_down, up, 0, margin + strip),
    ]

    def halo(side, target, source_row, target_row, plane, k):
        block = first + k
        return pltpu.make_async_remote_copy(
            src_ref=object_ref.at[plane, pl.ds(source_row, margin), pl.ds(pl.multiple_of(block * LANES, LANES), LANES)],
            dst_ref=ext_ref.at[plane, block, pl.ds(target_row, margin), :],
            send_sem=halo_send.at[side, plane, k],
            recv_sem=halo_recv.at[side, plane, k],
            device_id=device(target, mode),
            device_id_type=MESH,
        )

    def forward(side, target_row, plane, k, p):
        part = ext_ref.at[plane, first + k, pl.ds(target_row, margin), :]
        return pltpu.make_async_remote_copy(
            src_ref=part,
            dst_ref=part,
            send_sem=pass_send.at[p, side, plane, k],
            recv_sem=pass_recv.at[p, side, plane, k],
            device_id=device(tile, partners[p]),
            device_id_type=MESH,
        )

    def share_probe(p):
        return pltpu.make_async_remote_copy(
            src_ref=probe_ref.at[0],
            dst_ref=probes_ref.at[mode],
            send_sem=probe_send.at[p],
            recv_sem=probe_recv.at[p],
            device_id=device(tile, partners[p]),
            device_id_type=MESH,
        )

    pieces = [(plane, k) for plane in range(2) for k in range(share)]

    def send(plane, k):
        for side, sends, _, target, source_row, target_row in sides:

            @pl.when(sends)
            def _():
                halo(side, target, source_row, target_row, plane, k).start()

    for piece in pieces[:WINDOW]:
        send(*piece)
    for p in range(n_mode - 1):
        share_probe(p).start()

    for side, _, gets, _, _, target_row in sides:

        @pl.when(jnp.logical_not(gets))
        def _():
            ext_ref[:, :, pl.ds(target_row, margin), :] = jnp.zeros((2, blocks, margin, LANES), F32)

    for step, (plane, k) in enumerate(pieces):
        for side, _, gets, target, source_row, target_row in sides:

            @pl.when(gets)
            def _():
                halo(side, target, source_row, target_row, plane, k).wait_recv()
                for p in range(n_mode - 1):
                    forward(side, target_row, plane, k, p).start()

        for piece in pieces[step + WINDOW:step + WINDOW + 1]:
            send(*piece)

    for copy in local:
        copy.wait()
    for p in range(n_mode - 1):
        share_probe(p).wait()
    for plane in range(2):
        for k in range(share):
            for side, sends, gets, target, source_row, target_row in sides:

                @pl.when(gets)
                def _():
                    for p in range(n_mode - 1):
                        forward(side, target_row, plane, k, p).wait()

                @pl.when(sends)
                def _():
                    halo(side, target, source_row, target_row, plane, k).wait_send()


def exchange_halo(n_tile, n_mode, object_wave, probe, amplitudes, rows, columns_at):
    planes, strip, columns = object_wave.shape
    length = probe.shape[-1]
    blocks = columns // LANES
    share = blocks // n_mode
    peers = max(n_mode - 1, 1)
    dma = pltpu.SemaphoreType.DMA
    vmem = pl.BlockSpec(memory_space=pltpu.VMEM)
    hbm = pl.BlockSpec(memory_space=pltpu.HBM)
    table = tables(length)
    count = amplitudes.shape[0] // n_mode
    return pl.pallas_call(
        functools.partial(halo_kernel, n_tile, n_mode),
        out_shape=(
            jax.ShapeDtypeStruct((planes, blocks, strip + length, LANES), F32),
            jax.ShapeDtypeStruct((n_mode, 2, length, length), F32),
            jax.ShapeDtypeStruct((count,) + amplitudes.shape[1:], amplitudes.dtype),
            jax.ShapeDtypeStruct(rows.shape, rows.dtype),
            jax.ShapeDtypeStruct(columns_at.shape, columns_at.dtype),
            jax.ShapeDtypeStruct(table.shape, table.dtype),
        ),
        in_specs=[hbm] * 6,
        out_specs=(vmem,) * 6,
        scratch_shapes=[
            dma((2, 2, share)), dma((2, 2, share)),
            dma((peers, 2, 2, share)), dma((peers, 2, 2, share)),
            dma((peers,)), dma((peers,)), dma((2, blocks)), dma((5,)),
        ],
        compiler_params=pltpu.CompilerParams(
            collective_id=0, has_side_effects=True, vmem_limit_bytes=40 * 2**20
        ),
        name="halo",
    )(*[pltpu.with_memory_space_constraint(x, pltpu.HBM)
        for x in (object_wave, probe, amplitudes, rows, columns_at, table)])


def gradient_kernel(n_mode, rows_ref, columns_ref, ext_ref, probes_ref, amplitude_ref, table_ref,
                    canvas_ref, total_ref, spectra_ref):
    length = probes_ref.shape[-1]
    count = amplitude_ref.shape[0]
    forward_ref, adjoint_ref = table_ref.at[0], table_ref.at[1]
    blocks = ext_ref.shape[1]
    base = lax.axis_index("mode") * count
    canvas_ref[...] = jnp.zeros_like(canvas_ref)
    total_ref[...] = jnp.zeros_like(total_ref)
    lane = lax.broadcasted_iota(jnp.int32, (length, LANES), 1)
    pairs = [tuple(range(m, min(m + 2, n_mode))) for m in range(0, n_mode, 2)]

    def dot(a, b):
        return jnp.dot(a, b, preferred_element_type=F32)

    def halves(x, row_count):
        top = [x[:length, i * length:(i + 1) * length] for i in range(row_count)]
        low = [x[length:, i * length:(i + 1) * length] for i in range(row_count)]
        return jnp.concatenate([jnp.concatenate([a, b], axis=1) for a, b in zip(top, low)], axis=0)

    def step(index):
        row = rows_ref[base + index]
        column = columns_ref[base + index]
        block = lax.min(lax.shift_right_logical(column, 7), blocks - 2)
        shift = column - block * LANES
        back = lax.bitwise_and(LANES - shift, LANES - 1)
        ahead = lax.bitwise_and(shift, LANES - 1)

        def patch(plane):
            near = pltpu.roll(ext_ref[plane, block, pl.ds(row, length), :], back, 1)
            far = pltpu.roll(ext_ref[plane, block + 1, pl.ds(row, length), :], back, 1)
            return jnp.where(lane < LANES - shift, near, far)

        object_real, object_imag = patch(0), patch(1)
        intensity = jnp.zeros((length, length), F32)
        for number, pair in enumerate(pairs):
            reals, imags = [], []
            for m in pair:
                probe_real, probe_imag = probes_ref[m, 0], probes_ref[m, 1]
                reals.append((probe_real * object_real - probe_imag * object_imag).astype(BF16))
                imags.append((probe_real * object_imag + probe_imag * object_real).astype(BF16))
            wave = jnp.concatenate([jnp.concatenate(reals, axis=1), jnp.concatenate(imags, axis=1)], axis=0)
            half = dot(forward_ref[...], wave).astype(BF16)
            spectrum = dot(halves(half, len(pair)), adjoint_ref[...])
            for i in range(len(pair)):
                part = spectrum[i * length:(i + 1) * length]
                intensity += part[:, :length] * part[:, :length] + part[:, length:] * part[:, length:]
            if len(pairs) > 1:
                spectra_ref[number, :len(pair) * length] = spectrum
        amplitude = amplitude_ref[index].astype(F32)
        factor = 1.0 - amplitude * lax.rsqrt(jnp.maximum(intensity, FLOOR))
        term_real = jnp.zeros((length, length), F32)
        term_imag = jnp.zeros((length, length), F32)
        for number, pair in enumerate(pairs):
            if len(pairs) > 1:
                spectrum = spectra_ref[number, :len(pair) * length]
            reals, imags = [], []
            for i in range(len(pair)):
                part = spectrum[i * length:(i + 1) * length]
                reals.append((factor * part[:, :length]).astype(BF16))
                imags.append((factor * part[:, length:]).astype(BF16))
            chi = jnp.concatenate([jnp.concatenate(reals, axis=1), jnp.concatenate(imags, axis=1)], axis=0)
            half = dot(adjoint_ref[...], chi).astype(BF16)
            result = dot(halves(half, len(pair)), forward_ref[...])
            for i, m in enumerate(pair):
                real = result[i * length:(i + 1) * length, :length]
                imag = result[i * length:(i + 1) * length, length:]
                probe_real, probe_imag = probes_ref[m, 0], probes_ref[m, 1]
                term_real += probe_real * real + probe_imag * imag
                term_imag += probe_real * imag - probe_imag * real
                total_ref[m, 0] += object_real * real + object_imag * imag
                total_ref[m, 1] += object_real * imag - object_imag * real
        for plane, term in ((0, term_real), (1, term_imag)):
            moved = pltpu.roll(term, ahead, 1)
            canvas_ref[plane, block, pl.ds(row, length), :] += jnp.where(lane >= shift, moved, 0.0)
            canvas_ref[plane, block + 1, pl.ds(row, length), :] += jnp.where(lane < shift, moved, 0.0)

    @pl.loop(0, count, unroll=4)
    def _(index):
        step(index)


def gradients(n_mode, ext, probes, amplitudes, rows, columns, table):
    length = probes.shape[-1]
    vmem = pl.BlockSpec(memory_space=pltpu.VMEM)
    smem = pl.BlockSpec(memory_space=pltpu.SMEM)
    return pl.pallas_call(
        functools.partial(gradient_kernel, n_mode),
        out_shape=(
            jax.ShapeDtypeStruct(ext.shape, F32),
            jax.ShapeDtypeStruct(probes.shape, F32),
        ),
        in_specs=[smem, smem, vmem, vmem, vmem, vmem],
        out_specs=(vmem, vmem),
        scratch_shapes=[pltpu.VMEM(((n_mode + 1) // 2, 2 * length, 2 * length), F32)],
        compiler_params=pltpu.CompilerParams(vmem_limit_bytes=40 * 2**20),
        name="gradient",
    )(rows, columns, ext, probes, amplitudes, table)


def sum_kernel(n_tile, n_mode, canvas_ref, partial_ref, object_ref, probe_ref,
               landed, rim_out, rim_in, probe_in, probe_own, chunks_in, half_out, half_in,
               mode_send, mode_recv, rim_send, rim_recv, part_send, part_recv,
               scatter_send, scatter_recv, gather_send, gather_recv, twin_send, twin_recv):
    tile, mode = lax.axis_index("tile"), lax.axis_index("mode")
    strip = object_ref.shape[1]
    extent = canvas_ref.shape[2]
    margin = (extent - strip) // 2
    share = landed.shape[2]
    chunk = chunks_in.shape[1]
    reducers = probe_own.shape[0] // chunk
    group = n_tile // 2
    parity, member = lax.rem(tile, 2), tile // 2
    twin = tile + 1 - 2 * parity
    has_up, has_down = tile > 0, tile < n_tile - 1
    up, down = lax.max(tile - 1, 0), lax.min(tile + 1, n_tile - 1)
    partners = [lax.rem(mode + k, n_mode) for k in range(1, n_mode)]

    def peer(k):
        number = lax.rem(member + k, group)
        return number, 2 * number + parity

    barrier = pltpu.get_barrier_semaphore()
    for partner in partners:
        pl.semaphore_signal(barrier, inc=1, device_id=device(tile, partner), device_id_type=MESH)

    @pl.when(has_up)
    def _():
        pl.semaphore_signal(barrier, inc=1, device_id=device(up, mode), device_id_type=MESH)

    @pl.when(has_down)
    def _():
        pl.semaphore_signal(barrier, inc=1, device_id=device(down, mode), device_id_type=MESH)

    @pl.loop(1, group)
    def _(k):
        pl.semaphore_signal(barrier, inc=1, device_id=device(peer(k)[1], mode), device_id_type=MESH)

    signals = n_mode - 1 + group - 1 + has_up.astype(jnp.int32) + has_down.astype(jnp.int32)
    pl.semaphore_wait(barrier, signals)

    half = max(share // 2, 1)
    pieces = [(plane, low, half) for plane in range(2) for low in range(0, share, half)]

    sections = [(0, margin), (margin + strip, margin), (margin, strip)]

    def to_mode(p, section, plane):
        start, size = sections[section]
        return pltpu.make_async_remote_copy(
            src_ref=canvas_ref.at[plane, pl.ds(partners[p] * share, share), pl.ds(start, size), :],
            dst_ref=landed.at[p, plane, :, pl.ds(start, size), :],
            send_sem=mode_send.at[p, section, plane],
            recv_sem=mode_recv.at[p, section, plane],
            device_id=device(tile, partners[p]),
            device_id_type=MESH,
        )

    def part_to_mode(p):
        return pltpu.make_async_remote_copy(
            src_ref=partial_ref.at[partners[p]],
            dst_ref=probe_in.at[p],
            send_sem=part_send.at[p],
            recv_sem=part_recv.at[p],
            device_id=device(tile, partners[p]),
            device_id_type=MESH,
        )

    def rim(side, piece):
        plane, low, size = pieces[piece]
        return pltpu.make_async_remote_copy(
            src_ref=rim_out.at[side, plane, pl.ds(low, size)],
            dst_ref=rim_in.at[side, plane, pl.ds(low, size)],
            send_sem=rim_send.at[side, piece],
            recv_sem=rim_recv.at[side, piece],
            device_id=device(up if side == 0 else down, mode),
            device_id_type=MESH,
        )

    for p in range(n_mode - 1):
        part_to_mode(p).start()
    for plane in range(2):
        for section in (0, 1):
            for p in range(n_mode - 1):
                to_mode(p, section, plane).start()
    for plane in range(2):
        for p in range(n_mode - 1):
            to_mode(p, 2, plane).start()

    own_part = partial_ref[mode]
    for p in range(n_mode - 1):
        part_to_mode(p).wait_recv()
        own_part += probe_in[p]
    probe_own[...] = own_part.reshape(probe_own.shape)

    def rows_of(number):
        return pl.ds(pl.multiple_of(lax.rem(number, reducers) * chunk, chunk), chunk)

    def scatter(k):
        number, target = peer(k)
        return number, pltpu.make_async_remote_copy(
            src_ref=probe_own.at[rows_of(number), :],
            dst_ref=chunks_in.at[k - 1],
            send_sem=scatter_send.at[k - 1],
            recv_sem=scatter_recv.at[k - 1],
            device_id=device(target, mode),
            device_id_type=MESH,
        )

    @pl.loop(1, group)
    def _(k):
        number, copy = scatter(k)

        @pl.when(number < reducers)
        def _():
            copy.start()

    mine = pl.ds(mode * share, share)

    def sum_rims(plane):
        for section in (0, 1):
            start, size = sections[section]
            value = canvas_ref[plane, mine, start:start + size, :]
            for p in range(n_mode - 1):
                to_mode(p, section, plane).wait_recv()
                value += landed[p, plane, :, start:start + size, :]
            rim_out[section, plane] = value

    def send_rims(first, end):
        for piece in range(first, end):
            for section, sends in ((0, has_up), (1, has_down)):

                @pl.when(sends)
                def _():
                    rim(section, piece).start()

    count = len(pieces)
    sum_rims(0)
    send_rims(0, count // 2)
    sum_rims(1)

    start, size = sections[2]
    for plane in range(2):
        value = canvas_ref[plane, mine, start:start + size, :]
        for p in range(n_mode - 1):
            to_mode(p, 2, plane).wait_recv()
            value += landed[p, plane, :, start:start + size, :]
        for k in range(share):
            object_ref[plane, :, k * LANES:(k + 1) * LANES] = value[k]

    to_twin = pltpu.make_async_remote_copy(
        src_ref=half_out, dst_ref=half_in, send_sem=twin_send, recv_sem=twin_recv,
        device_id=device(twin, mode), device_id_type=MESH,
    )

    def gather(k):
        return pltpu.make_async_remote_copy(
            src_ref=probe_ref.at[rows_of(member), :],
            dst_ref=probe_ref.at[rows_of(member), :],
            send_sem=gather_send.at[k - 1],
            recv_sem=gather_recv.at[k - 1],
            device_id=device(peer(k)[1], mode),
            device_id_type=MESH,
        )

    @pl.when(member < reducers)
    def _():
        @pl.loop(1, group)
        def _(k):
            scatter(k)[1].wait_recv()

        value = probe_own[rows_of(member), :]
        for k in range(group - 1):
            value += chunks_in[k]
        half_out[...] = value
        to_twin.start()

    send_rims(count // 2, 3 * count // 4)

    @pl.when(member < reducers)
    def _():
        to_twin.wait_recv()
        probe_ref[rows_of(member), :] = half_out[...] + half_in[...]

        @pl.loop(1, group)
        def _(k):
            gather(k).start()

    send_rims(3 * count // 4, count)
    for piece, (plane, low, blocks) in enumerate(pieces):
        for side, gets, row in ((0, has_down, strip - margin), (1, has_up, 0)):

            @pl.when(gets)
            def _():
                rim(side, piece).wait_recv()
                for k in range(low, low + blocks):
                    object_ref[plane, row:row + margin, k * LANES:(k + 1) * LANES] += rim_in[side, plane, k]

    @pl.loop(1, group)
    def _(k):
        @pl.when(lax.rem(member + group - k, group) < reducers)
        def _():
            gather(k).wait_recv()

        number, copy = scatter(k)

        @pl.when(number < reducers)
        def _():
            copy.wait_send()

        @pl.when(member < reducers)
        def _():
            gather(k).wait_send()

    @pl.when(member < reducers)
    def _():
        to_twin.wait_send()

    for p in range(n_mode - 1):
        part_to_mode(p).wait_send()
        for section in range(3):
            for plane in range(2):
                to_mode(p, section, plane).wait_send()
    for section, sends in ((0, has_up), (1, has_down)):

        @pl.when(sends)
        def _():
            for piece in range(count):
                rim(section, piece).wait_send()


def sum_gradients(n_tile, n_mode, canvas, partial, margin):
    planes, blocks, extent, _ = canvas.shape
    length = partial.shape[-1]
    share = blocks // n_mode
    strip = extent - 2 * margin
    peers = max(n_mode - 1, 1)
    pieces = planes * (share // max(share // 2, 1))
    chunk = max(2 * length // (n_tile // 2), 8)
    dma = pltpu.SemaphoreType.DMA
    vmem = pl.BlockSpec(memory_space=pltpu.VMEM)
    others = n_tile // 2 - 1
    object_grad, probe_grad = pl.pallas_call(
        functools.partial(sum_kernel, n_tile, n_mode),
        out_shape=(
            jax.ShapeDtypeStruct((planes, strip, share * LANES), F32),
            jax.ShapeDtypeStruct((2 * length, length), F32),
        ),
        in_specs=[vmem, vmem],
        out_specs=(vmem, vmem),
        scratch_shapes=[
            pltpu.VMEM((peers, planes, share, extent, LANES), F32),
            pltpu.VMEM((2, planes, share, margin, LANES), F32),
            pltpu.VMEM((2, planes, share, margin, LANES), F32),
            pltpu.VMEM((peers, 2, length, length), F32),
            pltpu.VMEM((2 * length, length), F32),
            pltpu.VMEM((others, chunk, length), F32),
            pltpu.VMEM((chunk, length), F32),
            pltpu.VMEM((chunk, length), F32),
            dma((peers, 3, planes)), dma((peers, 3, planes)),
            dma((2, pieces)), dma((2, pieces)),
            dma((peers,)), dma((peers,)),
            dma((others,)), dma((others,)), dma((others,)), dma((others,)), dma, dma,
        ],
        compiler_params=pltpu.CompilerParams(
            collective_id=1, has_side_effects=True, vmem_limit_bytes=40 * 2**20
        ),
        name="sums",
    )(canvas, partial)
    return object_grad, probe_grad.reshape(1, 2, length, length)


def solution(mesh):
    n_tile, n_mode = mesh.shape["tile"], mesh.shape["mode"]

    def body(object_wave, probe, amplitudes, rows, columns):
        held = exchange_halo(n_tile, n_mode, object_wave, probe, amplitudes, rows, columns)
        canvas, partial = gradients(n_mode, *held)
        return sum_gradients(n_tile, n_mode, canvas, partial, probe.shape[-1] // 2)

    placed = (
        P(None, "tile", None),
        P("mode", None, None, None),
        P("tile", None, None),
        P("tile"),
        P("tile"),
    )
    return jax.shard_map(
        body,
        mesh=mesh,
        in_specs=placed,
        out_specs=(P(None, "tile", "mode"), P("mode", None, None, None)),
        check_vma=False,
    )
```

```python
import functools
import jax
import jax.numpy as jnp
import numpy as np
from jax import lax
from jax.experimental import pallas as pl
from jax.experimental.pallas import tpu as pltpu
from jax.sharding import PartitionSpec as P

FLOOR = 0.25
LANES = 128
WINDOW = 8
MESH = pl.DeviceIdType.MESH
F32 = jnp.float32
BF16 = jnp.bfloat16


def tables(length):
    index = np.arange(length, dtype=np.int64)
    angle = (index[:, None] * index[None, :] % length) * (2.0 * np.pi / length)
    cosine, sine = np.cos(angle) / np.sqrt(length), np.sin(angle) / np.sqrt(length)
    forward = np.block([[cosine, sine], [-sine, cosine]])
    adjoint = np.block([[cosine, -sine], [sine, cosine]])
    return jnp.asarray(np.stack([forward, adjoint]), dtype=BF16)


def device(tile, mode):
    return (tile, mode)


def halo_kernel(n_tile, n_mode, object_ref, probe_ref, amplitude_ref, rows_ref, columns_ref, table_ref,
                ext_ref, probes_ref, amplitude_out, rows_out, columns_out, table_out,
                halo_send, halo_recv, pass_send, pass_recv, probe_send, probe_recv, local_sem, own_sem):
    tile, mode = lax.axis_index("tile"), lax.axis_index("mode")
    strip = object_ref.shape[1]
    margin = (ext_ref.shape[2] - strip) // 2
    blocks = ext_ref.shape[1]
    share = blocks // n_mode
    first = mode * share
    has_up, has_down = tile > 0, tile < n_tile - 1
    up, down = lax.max(tile - 1, 0), lax.min(tile + 1, n_tile - 1)
    partners = [lax.rem(mode + k, n_mode) for k in range(1, n_mode)]

    barrier = pltpu.get_barrier_semaphore()
    for partner in partners:
        pl.semaphore_signal(barrier, inc=1, device_id=device(tile, partner), device_id_type=MESH)

    @pl.when(has_up)
    def _():
        pl.semaphore_signal(barrier, inc=1, device_id=device(up, mode), device_id_type=MESH)

    @pl.when(has_down)
    def _():
        pl.semaphore_signal(barrier, inc=1, device_id=device(down, mode), device_id_type=MESH)

    local = []
    for plane in range(2):
        for block in range(blocks):
            copy = pltpu.make_async_copy(
                object_ref.at[plane, :, pl.ds(block * LANES, LANES)],
                ext_ref.at[plane, block, pl.ds(margin, strip), :],
                local_sem.at[plane, block],
            )
            copy.start()
            local.append(copy)
    count = amplitude_out.shape[0]
    held = [
        (probe_ref.at[0], probes_ref.at[mode]),
        (amplitude_ref.at[pl.ds(mode * count, count)], amplitude_out),
        (rows_ref, rows_out),
        (columns_ref, columns_out),
        (table_ref, table_out),
    ]
    for number, (source, target) in enumerate(held):
        copy = pltpu.make_async_copy(source, target, own_sem.at[number])
        copy.start()
        local.append(copy)
    pl.semaphore_wait(barrier, n_mode - 1 + has_up.astype(jnp.int32) + has_down.astype(jnp.int32))

    sides = [
        (0, has_down, has_up, down, strip - margin, 0),
        (1, has_up, has_down, up, 0, margin + strip),
    ]

    def halo(side, target, source_row, target_row, plane, k):
        block = first + k
        return pltpu.make_async_remote_copy(
            src_ref=object_ref.at[plane, pl.ds(source_row, margin), pl.ds(pl.multiple_of(block * LANES, LANES), LANES)],
            dst_ref=ext_ref.at[plane, block, pl.ds(target_row, margin), :],
            send_sem=halo_send.at[side, plane, k],
            recv_sem=halo_recv.at[side, plane, k],
            device_id=device(target, mode),
            device_id_type=MESH,
        )

    def forward(side, target_row, plane, k, p):
        part = ext_ref.at[plane, first + k, pl.ds(target_row, margin), :]
        return pltpu.make_async_remote_copy(
            src_ref=part,
            dst_ref=part,
            send_sem=pass_send.at[p, side, plane, k],
            recv_sem=pass_recv.at[p, side, plane, k],
            device_id=device(tile, partners[p]),
            device_id_type=MESH,
        )

    def share_probe(p):
        return pltpu.make_async_remote_copy(
            src_ref=probe_ref.at[0],
            dst_ref=probes_ref.at[mode],
            send_sem=probe_send.at[p],
            recv_sem=probe_recv.at[p],
            device_id=device(tile, partners[p]),
            device_id_type=MESH,
        )

    pieces = [(plane, k) for plane in range(2) for k in range(share)]

    def send(plane, k):
        for side, sends, _, target, source_row, target_row in sides:

            @pl.when(sends)
            def _():
                halo(side, target, source_row, target_row, plane, k).start()

    for piece in pieces[:WINDOW]:
        send(*piece)
    for p in range(n_mode - 1):
        share_probe(p).start()

    for side, _, gets, _, _, target_row in sides:

        @pl.when(jnp.logical_not(gets))
        def _():
            ext_ref[:, :, pl.ds(target_row, margin), :] = jnp.zeros((2, blocks, margin, LANES), F32)

    for step, (plane, k) in enumerate(pieces):
        for side, _, gets, target, source_row, target_row in sides:

            @pl.when(gets)
            def _():
                halo(side, target, source_row, target_row, plane, k).wait_recv()
                for p in range(n_mode - 1):
                    forward(side, target_row, plane, k, p).start()

        for piece in pieces[step + WINDOW:step + WINDOW + 1]:
            send(*piece)

    for copy in local:
        copy.wait()
    for p in range(n_mode - 1):
        share_probe(p).wait()
    for plane in range(2):
        for k in range(share):
            for side, sends, gets, target, source_row, target_row in sides:

                @pl.when(gets)
                def _():
                    for p in range(n_mode - 1):
                        forward(side, target_row, plane, k, p).wait()

                @pl.when(sends)
                def _():
                    halo(side, target, source_row, target_row, plane, k).wait_send()


def exchange_halo(n_tile, n_mode, object_wave, probe, amplitudes, rows, columns_at):
    planes, strip, columns = object_wave.shape
    length = probe.shape[-1]
    blocks = columns // LANES
    share = blocks // n_mode
    peers = max(n_mode - 1, 1)
    dma = pltpu.SemaphoreType.DMA
    vmem = pl.BlockSpec(memory_space=pltpu.VMEM)
    hbm = pl.BlockSpec(memory_space=pltpu.HBM)
    table = tables(length)
    count = amplitudes.shape[0] // n_mode
    return pl.pallas_call(
        functools.partial(halo_kernel, n_tile, n_mode),
        out_shape=(
            jax.ShapeDtypeStruct((planes, blocks, strip + length, LANES), F32),
            jax.ShapeDtypeStruct((n_mode, 2, length, length), F32),
            jax.ShapeDtypeStruct((count,) + amplitudes.shape[1:], amplitudes.dtype),
            jax.ShapeDtypeStruct(rows.shape, rows.dtype),
            jax.ShapeDtypeStruct(columns_at.shape, columns_at.dtype),
            jax.ShapeDtypeStruct(table.shape, table.dtype),
        ),
        in_specs=[hbm] * 6,
        out_specs=(vmem,) * 6,
        scratch_shapes=[
            dma((2, 2, share)), dma((2, 2, share)),
            dma((peers, 2, 2, share)), dma((peers, 2, 2, share)),
            dma((peers,)), dma((peers,)), dma((2, blocks)), dma((5,)),
        ],
        compiler_params=pltpu.CompilerParams(
            collective_id=0, has_side_effects=True, vmem_limit_bytes=40 * 2**20
        ),
        name="halo",
    )(*[pltpu.with_memory_space_constraint(x, pltpu.HBM)
        for x in (object_wave, probe, amplitudes, rows, columns_at, table)])


def gradient_kernel(n_mode, rows_ref, columns_ref, ext_ref, probes_ref, amplitude_ref, table_ref,
                    canvas_ref, total_ref, spectra_ref):
    length = probes_ref.shape[-1]
    count = amplitude_ref.shape[0]
    forward_ref, adjoint_ref = table_ref.at[0], table_ref.at[1]
    blocks = ext_ref.shape[1]
    base = lax.axis_index("mode") * count
    canvas_ref[...] = jnp.zeros_like(canvas_ref)
    total_ref[...] = jnp.zeros_like(total_ref)
    lane = lax.broadcasted_iota(jnp.int32, (length, LANES), 1)
    pairs = [tuple(range(m, min(m + 2, n_mode))) for m in range(0, n_mode, 2)]

    def dot(a, b):
        return jnp.dot(a, b, preferred_element_type=F32)

    def halves(x, row_count):
        top = [x[:length, i * length:(i + 1) * length] for i in range(row_count)]
        low = [x[length:, i * length:(i + 1) * length] for i in range(row_count)]
        return jnp.concatenate([jnp.concatenate([a, b], axis=1) for a, b in zip(top, low)], axis=0)

    def step(index):
        row = rows_ref[base + index]
        column = columns_ref[base + index]
        block = lax.min(lax.shift_right_logical(column, 7), blocks - 2)
        shift = column - block * LANES
        back = lax.bitwise_and(LANES - shift, LANES - 1)
        ahead = lax.bitwise_and(shift, LANES - 1)

        def patch(plane):
            near = pltpu.roll(ext_ref[plane, block, pl.ds(row, length), :], back, 1)
            far = pltpu.roll(ext_ref[plane, block + 1, pl.ds(row, length), :], back, 1)
            return jnp.where(lane < LANES - shift, near, far)

        object_real, object_imag = patch(0), patch(1)
        intensity = jnp.zeros((length, length), F32)
        for number, pair in enumerate(pairs):
            reals, imags = [], []
            for m in pair:
                probe_real, probe_imag = probes_ref[m, 0], probes_ref[m, 1]
                reals.append((probe_real * object_real - probe_imag * object_imag).astype(BF16))
                imags.append((probe_real * object_imag + probe_imag * object_real).astype(BF16))
            wave = jnp.concatenate([jnp.concatenate(reals, axis=1), jnp.concatenate(imags, axis=1)], axis=0)
            half = dot(forward_ref[...], wave).astype(BF16)
            spectrum = dot(halves(half, len(pair)), adjoint_ref[...])
            for i in range(len(pair)):
                part = spectrum[i * length:(i + 1) * length]
                intensity += part[:, :length] * part[:, :length] + part[:, length:] * part[:, length:]
            if len(pairs) > 1:
                spectra_ref[number, :len(pair) * length] = spectrum
        amplitude = amplitude_ref[index].astype(F32)
        factor = 1.0 - amplitude * lax.rsqrt(jnp.maximum(intensity, FLOOR))
        term_real = jnp.zeros((length, length), F32)
        term_imag = jnp.zeros((length, length), F32)
        for number, pair in enumerate(pairs):
            if len(pairs) > 1:
                spectrum = spectra_ref[number, :len(pair) * length]
            reals, imags = [], []
            for i in range(len(pair)):
                part = spectrum[i * length:(i + 1) * length]
                reals.append((factor * part[:, :length]).astype(BF16))
                imags.append((factor * part[:, length:]).astype(BF16))
            chi = jnp.concatenate([jnp.concatenate(reals, axis=1), jnp.concatenate(imags, axis=1)], axis=0)
            half = dot(adjoint_ref[...], chi).astype(BF16)
            result = dot(halves(half, len(pair)), forward_ref[...])
            for i, m in enumerate(pair):
                real = result[i * length:(i + 1) * length, :length]
                imag = result[i * length:(i + 1) * length, length:]
                probe_real, probe_imag = probes_ref[m, 0], probes_ref[m, 1]
                term_real += probe_real * real + probe_imag * imag
                term_imag += probe_real * imag - probe_imag * real
                total_ref[m, 0] += object_real * real + object_imag * imag
                total_ref[m, 1] += object_real * imag - object_imag * real
        for plane, term in ((0, term_real), (1, term_imag)):
            moved = pltpu.roll(term, ahead, 1)
            canvas_ref[plane, block, pl.ds(row, length), :] += jnp.where(lane >= shift, moved, 0.0)
            canvas_ref[plane, block + 1, pl.ds(row, length), :] += jnp.where(lane < shift, moved, 0.0)

    @pl.loop(0, count, unroll=8 if count % 8 == 0 else 2)
    def _(index):
        step(index)


def gradients(n_mode, ext, probes, amplitudes, rows, columns, table):
    length = probes.shape[-1]
    vmem = pl.BlockSpec(memory_space=pltpu.VMEM)
    smem = pl.BlockSpec(memory_space=pltpu.SMEM)
    return pl.pallas_call(
        functools.partial(gradient_kernel, n_mode),
        out_shape=(
            jax.ShapeDtypeStruct(ext.shape, F32),
            jax.ShapeDtypeStruct(probes.shape, F32),
        ),
        in_specs=[smem, smem, vmem, vmem, vmem, vmem],
        out_specs=(vmem, vmem),
        scratch_shapes=[pltpu.VMEM(((n_mode + 1) // 2, 2 * length, 2 * length), F32)],
        compiler_params=pltpu.CompilerParams(vmem_limit_bytes=40 * 2**20),
        name="gradient",
    )(rows, columns, ext, probes, amplitudes, table)


def sum_kernel(n_tile, n_mode, canvas_ref, partial_ref, object_ref, probe_ref,
               landed, rim_out, rim_in, probe_in, probe_own, chunks_in, half_out, half_in,
               mode_send, mode_recv, rim_send, rim_recv, part_send, part_recv,
               scatter_send, scatter_recv, gather_send, gather_recv, twin_send, twin_recv):
    tile, mode = lax.axis_index("tile"), lax.axis_index("mode")
    strip = object_ref.shape[1]
    extent = canvas_ref.shape[2]
    margin = (extent - strip) // 2
    share = landed.shape[2]
    chunk = chunks_in.shape[1]
    reducers = probe_own.shape[0] // chunk
    group = n_tile // 2
    parity, member = lax.rem(tile, 2), tile // 2
    twin = tile + 1 - 2 * parity
    has_up, has_down = tile > 0, tile < n_tile - 1
    up, down = lax.max(tile - 1, 0), lax.min(tile + 1, n_tile - 1)
    partners = [lax.rem(mode + k, n_mode) for k in range(1, n_mode)]

    def peer(k):
        number = lax.rem(member + k, group)
        return number, 2 * number + parity

    barrier = pltpu.get_barrier_semaphore()
    for partner in partners:
        pl.semaphore_signal(barrier, inc=1, device_id=device(tile, partner), device_id_type=MESH)

    @pl.when(has_up)
    def _():
        pl.semaphore_signal(barrier, inc=1, device_id=device(up, mode), device_id_type=MESH)

    @pl.when(has_down)
    def _():
        pl.semaphore_signal(barrier, inc=1, device_id=device(down, mode), device_id_type=MESH)

    @pl.loop(1, group)
    def _(k):
        pl.semaphore_signal(barrier, inc=1, device_id=device(peer(k)[1], mode), device_id_type=MESH)

    signals = n_mode - 1 + group - 1 + has_up.astype(jnp.int32) + has_down.astype(jnp.int32)
    pl.semaphore_wait(barrier, signals)

    half = max(share // 2, 1)
    pieces = [(plane, low, half) for plane in range(2) for low in range(0, share, half)]

    sections = [(0, margin), (margin + strip, margin), (margin, strip)]

    def to_mode(p, section, plane):
        start, size = sections[section]
        return pltpu.make_async_remote_copy(
            src_ref=canvas_ref.at[plane, pl.ds(partners[p] * share, share), pl.ds(start, size), :],
            dst_ref=landed.at[p, plane, :, pl.ds(start, size), :],
            send_sem=mode_send.at[p, section, plane],
            recv_sem=mode_recv.at[p, section, plane],
            device_id=device(tile, partners[p]),
            device_id_type=MESH,
        )

    def part_to_mode(p):
        return pltpu.make_async_remote_copy(
            src_ref=partial_ref.at[partners[p]],
            dst_ref=probe_in.at[p],
            send_sem=part_send.at[p],
            recv_sem=part_recv.at[p],
            device_id=device(tile, partners[p]),
            device_id_type=MESH,
        )

    def rim(side, piece):
        plane, low, size = pieces[piece]
        return pltpu.make_async_remote_copy(
            src_ref=rim_out.at[side, plane, pl.ds(low, size)],
            dst_ref=rim_in.at[side, plane, pl.ds(low, size)],
            send_sem=rim_send.at[side, piece],
            recv_sem=rim_recv.at[side, piece],
            device_id=device(up if side == 0 else down, mode),
            device_id_type=MESH,
        )

    for p in range(n_mode - 1):
        part_to_mode(p).start()
    for plane in range(2):
        for section in (0, 1):
            for p in range(n_mode - 1):
                to_mode(p, section, plane).start()
    for plane in range(2):
        for p in range(n_mode - 1):
            to_mode(p, 2, plane).start()

    own_part = partial_ref[mode]
    for p in range(n_mode - 1):
        part_to_mode(p).wait_recv()
        own_part += probe_in[p]
    probe_own[...] = own_part.reshape(probe_own.shape)

    def rows_of(number):
        return pl.ds(pl.multiple_of(lax.rem(number, reducers) * chunk, chunk), chunk)

    def scatter(k):
        number, target = peer(k)
        return number, pltpu.make_async_remote_copy(
            src_ref=probe_own.at[rows_of(number), :],
            dst_ref=chunks_in.at[k - 1],
            send_sem=scatter_send.at[k - 1],
            recv_sem=scatter_recv.at[k - 1],
            device_id=device(target, mode),
            device_id_type=MESH,
        )

    @pl.loop(1, group)
    def _(k):
        number, copy = scatter(k)

        @pl.when(number < reducers)
        def _():
            copy.start()

    mine = pl.ds(mode * share, share)

    def sum_rims(plane):
        for section in (0, 1):
            start, size = sections[section]
            value = canvas_ref[plane, mine, start:start + size, :]
            for p in range(n_mode - 1):
                to_mode(p, section, plane).wait_recv()
                value += landed[p, plane, :, start:start + size, :]
            rim_out[section, plane] = value

    def send_rims(first, end):
        for piece in range(first, end):
            for section, sends in ((0, has_up), (1, has_down)):

                @pl.when(sends)
                def _():
                    rim(section, piece).start()

    count = len(pieces)
    sum_rims(0)
    send_rims(0, count // 2)
    sum_rims(1)

    start, size = sections[2]
    for plane in range(2):
        value = canvas_ref[plane, mine, start:start + size, :]
        for p in range(n_mode - 1):
            to_mode(p, 2, plane).wait_recv()
            value += landed[p, plane, :, start:start + size, :]
        for k in range(share):
            object_ref[plane, :, k * LANES:(k + 1) * LANES] = value[k]

    to_twin = pltpu.make_async_remote_copy(
        src_ref=half_out, dst_ref=half_in, send_sem=twin_send, recv_sem=twin_recv,
        device_id=device(twin, mode), device_id_type=MESH,
    )

    def gather(k):
        return pltpu.make_async_remote_copy(
            src_ref=probe_ref.at[rows_of(member), :],
            dst_ref=probe_ref.at[rows_of(member), :],
            send_sem=gather_send.at[k - 1],
            recv_sem=gather_recv.at[k - 1],
            device_id=device(peer(k)[1], mode),
            device_id_type=MESH,
        )

    @pl.when(member < reducers)
    def _():
        @pl.loop(1, group)
        def _(k):
            scatter(k)[1].wait_recv()

        value = probe_own[rows_of(member), :]
        for k in range(group - 1):
            value += chunks_in[k]
        half_out[...] = value
        to_twin.start()

    send_rims(count // 2, 3 * count // 4)

    @pl.when(member < reducers)
    def _():
        to_twin.wait_recv()
        probe_ref[rows_of(member), :] = half_out[...] + half_in[...]

        @pl.loop(1, group)
        def _(k):
            gather(k).start()

    send_rims(3 * count // 4, count)
    for piece, (plane, low, blocks) in enumerate(pieces):
        for side, gets, row in ((0, has_down, strip - margin), (1, has_up, 0)):

            @pl.when(gets)
            def _():
                rim(side, piece).wait_recv()
                for k in range(low, low + blocks):
                    object_ref[plane, row:row + margin, k * LANES:(k + 1) * LANES] += rim_in[side, plane, k]

    @pl.loop(1, group)
    def _(k):
        @pl.when(lax.rem(member + group - k, group) < reducers)
        def _():
            gather(k).wait_recv()

        number, copy = scatter(k)

        @pl.when(number < reducers)
        def _():
            copy.wait_send()

        @pl.when(member < reducers)
        def _():
            gather(k).wait_send()

    @pl.when(member < reducers)
    def _():
        to_twin.wait_send()

    for p in range(n_mode - 1):
        part_to_mode(p).wait_send()
        for section in range(3):
            for plane in range(2):
                to_mode(p, section, plane).wait_send()
    for section, sends in ((0, has_up), (1, has_down)):

        @pl.when(sends)
        def _():
            for piece in range(count):
                rim(section, piece).wait_send()


def sum_gradients(n_tile, n_mode, canvas, partial, margin):
    planes, blocks, extent, _ = canvas.shape
    length = partial.shape[-1]
    share = blocks // n_mode
    strip = extent - 2 * margin
    peers = max(n_mode - 1, 1)
    pieces = planes * (share // max(share // 2, 1))
    chunk = max(2 * length // (n_tile // 2), 8)
    dma = pltpu.SemaphoreType.DMA
    vmem = pl.BlockSpec(memory_space=pltpu.VMEM)
    others = n_tile // 2 - 1
    object_grad, probe_grad = pl.pallas_call(
        functools.partial(sum_kernel, n_tile, n_mode),
        out_shape=(
            jax.ShapeDtypeStruct((planes, strip, share * LANES), F32),
            jax.ShapeDtypeStruct((2 * length, length), F32),
        ),
        in_specs=[vmem, vmem],
        out_specs=(vmem, vmem),
        scratch_shapes=[
            pltpu.VMEM((peers, planes, share, extent, LANES), F32),
            pltpu.VMEM((2, planes, share, margin, LANES), F32),
            pltpu.VMEM((2, planes, share, margin, LANES), F32),
            pltpu.VMEM((peers, 2, length, length), F32),
            pltpu.VMEM((2 * length, length), F32),
            pltpu.VMEM((others, chunk, length), F32),
            pltpu.VMEM((chunk, length), F32),
            pltpu.VMEM((chunk, length), F32),
            dma((peers, 3, planes)), dma((peers, 3, planes)),
            dma((2, pieces)), dma((2, pieces)),
            dma((peers,)), dma((peers,)),
            dma((others,)), dma((others,)), dma((others,)), dma((others,)), dma, dma,
        ],
        compiler_params=pltpu.CompilerParams(
            collective_id=1, has_side_effects=True, vmem_limit_bytes=40 * 2**20
        ),
        name="sums",
    )(canvas, partial)
    return object_grad, probe_grad.reshape(1, 2, length, length)


def solution(mesh):
    n_tile, n_mode = mesh.shape["tile"], mesh.shape["mode"]

    def body(object_wave, probe, amplitudes, rows, columns):
        held = exchange_halo(n_tile, n_mode, object_wave, probe, amplitudes, rows, columns)
        canvas, partial = gradients(n_mode, *held)
        return sum_gradients(n_tile, n_mode, canvas, partial, probe.shape[-1] // 2)

    placed = (
        P(None, "tile", None),
        P("mode", None, None, None),
        P("tile", None, None),
        P("tile"),
        P("tile"),
    )
    return jax.shard_map(
        body,
        mesh=mesh,
        in_specs=placed,
        out_specs=(P(None, "tile", "mode"), P("mode", None, None, None)),
        check_vma=False,
    )
```

```python
import functools
import jax
import jax.numpy as jnp
import numpy as np
from jax import lax
from jax.experimental import pallas as pl
from jax.experimental.pallas import tpu as pltpu
from jax.sharding import PartitionSpec as P

FLOOR = 0.25
LANES = 128
WINDOW = 8
MESH = pl.DeviceIdType.MESH
F32 = jnp.float32
BF16 = jnp.bfloat16


def tables(length):
    index = np.arange(length, dtype=np.int64)
    angle = (index[:, None] * index[None, :] % length) * (2.0 * np.pi / length)
    cosine, sine = np.cos(angle) / np.sqrt(length), np.sin(angle) / np.sqrt(length)
    forward = np.block([[cosine, sine], [-sine, cosine]])
    adjoint = np.block([[cosine, -sine], [sine, cosine]])
    return jnp.asarray(np.stack([forward, adjoint]), dtype=BF16)


def device(tile, mode):
    return (tile, mode)


def halo_kernel(n_tile, n_mode, object_ref, probe_ref, amplitude_ref, rows_ref, columns_ref, table_ref,
                ext_ref, probes_ref, amplitude_out, rows_out, columns_out, table_out,
                halo_send, halo_recv, pass_send, pass_recv, probe_send, probe_recv, local_sem, own_sem):
    tile, mode = lax.axis_index("tile"), lax.axis_index("mode")
    strip = object_ref.shape[1]
    margin = (ext_ref.shape[2] - strip) // 2
    blocks = ext_ref.shape[1]
    share = blocks // n_mode
    first = mode * share
    has_up, has_down = tile > 0, tile < n_tile - 1
    up, down = lax.max(tile - 1, 0), lax.min(tile + 1, n_tile - 1)
    partners = [lax.rem(mode + k, n_mode) for k in range(1, n_mode)]

    barrier = pltpu.get_barrier_semaphore()
    for partner in partners:
        pl.semaphore_signal(barrier, inc=1, device_id=device(tile, partner), device_id_type=MESH)

    @pl.when(has_up)
    def _():
        pl.semaphore_signal(barrier, inc=1, device_id=device(up, mode), device_id_type=MESH)

    @pl.when(has_down)
    def _():
        pl.semaphore_signal(barrier, inc=1, device_id=device(down, mode), device_id_type=MESH)

    local = []
    for plane in range(2):
        for block in range(blocks):
            copy = pltpu.make_async_copy(
                object_ref.at[plane, :, pl.ds(block * LANES, LANES)],
                ext_ref.at[plane, block, pl.ds(margin, strip), :],
                local_sem.at[plane, block],
            )
            copy.start()
            local.append(copy)
    count = amplitude_out.shape[0]
    held = [
        (probe_ref.at[0], probes_ref.at[mode]),
        (amplitude_ref.at[pl.ds(mode * count, count)], amplitude_out),
        (rows_ref, rows_out),
        (columns_ref, columns_out),
        (table_ref, table_out),
    ]
    for number, (source, target) in enumerate(held):
        copy = pltpu.make_async_copy(source, target, own_sem.at[number])
        copy.start()
        local.append(copy)
    pl.semaphore_wait(barrier, n_mode - 1 + has_up.astype(jnp.int32) + has_down.astype(jnp.int32))

    sides = [
        (0, has_down, has_up, down, strip - margin, 0),
        (1, has_up, has_down, up, 0, margin + strip),
    ]

    def halo(side, target, source_row, target_row, plane, k):
        block = first + k
        return pltpu.make_async_remote_copy(
            src_ref=object_ref.at[plane, pl.ds(source_row, margin), pl.ds(pl.multiple_of(block * LANES, LANES), LANES)],
            dst_ref=ext_ref.at[plane, block, pl.ds(target_row, margin), :],
            send_sem=halo_send.at[side, plane, k],
            recv_sem=halo_recv.at[side, plane, k],
            device_id=device(target, mode),
            device_id_type=MESH,
        )

    def forward(side, target_row, plane, k, p):
        part = ext_ref.at[plane, first + k, pl.ds(target_row, margin), :]
        return pltpu.make_async_remote_copy(
            src_ref=part,
            dst_ref=part,
            send_sem=pass_send.at[p, side, plane, k],
            recv_sem=pass_recv.at[p, side, plane, k],
            device_id=device(tile, partners[p]),
            device_id_type=MESH,
        )

    def share_probe(p):
        return pltpu.make_async_remote_copy(
            src_ref=probe_ref.at[0],
            dst_ref=probes_ref.at[mode],
            send_sem=probe_send.at[p],
            recv_sem=probe_recv.at[p],
            device_id=device(tile, partners[p]),
            device_id_type=MESH,
        )

    pieces = [(plane, k) for plane in range(2) for k in range(share)]

    def send(plane, k):
        for side, sends, _, target, source_row, target_row in sides:

            @pl.when(sends)
            def _():
                halo(side, target, source_row, target_row, plane, k).start()

    for piece in pieces[:WINDOW]:
        send(*piece)
    for p in range(n_mode - 1):
        share_probe(p).start()

    for side, _, gets, _, _, target_row in sides:

        @pl.when(jnp.logical_not(gets))
        def _():
            ext_ref[:, :, pl.ds(target_row, margin), :] = jnp.zeros((2, blocks, margin, LANES), F32)

    for step, (plane, k) in enumerate(pieces):
        for side, _, gets, target, source_row, target_row in sides:

            @pl.when(gets)
            def _():
                halo(side, target, source_row, target_row, plane, k).wait_recv()
                for p in range(n_mode - 1):
                    forward(side, target_row, plane, k, p).start()

        for piece in pieces[step + WINDOW:step + WINDOW + 1]:
            send(*piece)

    for copy in local:
        copy.wait()
    for p in range(n_mode - 1):
        share_probe(p).wait()
    for plane in range(2):
        for k in range(share):
            for side, sends, gets, target, source_row, target_row in sides:

                @pl.when(gets)
                def _():
                    for p in range(n_mode - 1):
                        forward(side, target_row, plane, k, p).wait()

                @pl.when(sends)
                def _():
                    halo(side, target, source_row, target_row, plane, k).wait_send()


def exchange_halo(n_tile, n_mode, object_wave, probe, amplitudes, rows, columns_at):
    planes, strip, columns = object_wave.shape
    length = probe.shape[-1]
    blocks = columns // LANES
    share = blocks // n_mode
    peers = max(n_mode - 1, 1)
    dma = pltpu.SemaphoreType.DMA
    vmem = pl.BlockSpec(memory_space=pltpu.VMEM)
    hbm = pl.BlockSpec(memory_space=pltpu.HBM)
    table = tables(length)
    count = amplitudes.shape[0] // n_mode
    return pl.pallas_call(
        functools.partial(halo_kernel, n_tile, n_mode),
        out_shape=(
            jax.ShapeDtypeStruct((planes, blocks, strip + length, LANES), F32),
            jax.ShapeDtypeStruct((n_mode, 2, length, length), F32),
            jax.ShapeDtypeStruct((count,) + amplitudes.shape[1:], amplitudes.dtype),
            jax.ShapeDtypeStruct(rows.shape, rows.dtype),
            jax.ShapeDtypeStruct(columns_at.shape, columns_at.dtype),
            jax.ShapeDtypeStruct(table.shape, table.dtype),
        ),
        in_specs=[hbm] * 6,
        out_specs=(vmem,) * 6,
        scratch_shapes=[
            dma((2, 2, share)), dma((2, 2, share)),
            dma((peers, 2, 2, share)), dma((peers, 2, 2, share)),
            dma((peers,)), dma((peers,)), dma((2, blocks)), dma((5,)),
        ],
        compiler_params=pltpu.CompilerParams(
            collective_id=0, has_side_effects=True, vmem_limit_bytes=40 * 2**20
        ),
        name="halo",
    )(*[pltpu.with_memory_space_constraint(x, pltpu.HBM)
        for x in (object_wave, probe, amplitudes, rows, columns_at, table)])


def gradient_kernel(n_mode, rows_ref, columns_ref, ext_ref, probes_ref, amplitude_ref, table_ref,
                    canvas_ref, total_ref, spectra_ref):
    length = probes_ref.shape[-1]
    count = amplitude_ref.shape[0]
    forward_ref, adjoint_ref = table_ref.at[0], table_ref.at[1]
    blocks = ext_ref.shape[1]
    base = lax.axis_index("mode") * count
    canvas_ref[...] = jnp.zeros_like(canvas_ref)
    total_ref[...] = jnp.zeros_like(total_ref)
    lane = lax.broadcasted_iota(jnp.int32, (length, LANES), 1)
    pairs = [tuple(range(m, min(m + 2, n_mode))) for m in range(0, n_mode, 2)]

    def dot(a, b):
        return jnp.dot(a, b, preferred_element_type=F32)

    def halves(x, row_count):
        top = [x[:length, i * length:(i + 1) * length] for i in range(row_count)]
        low = [x[length:, i * length:(i + 1) * length] for i in range(row_count)]
        return jnp.concatenate([jnp.concatenate([a, b], axis=1) for a, b in zip(top, low)], axis=0)

    def step(index):
        row = rows_ref[base + index]
        column = columns_ref[base + index]
        block = lax.min(lax.shift_right_logical(column, 7), blocks - 2)
        shift = column - block * LANES
        back = lax.bitwise_and(LANES - shift, LANES - 1)
        ahead = lax.bitwise_and(shift, LANES - 1)

        def patch(plane):
            near = pltpu.roll(ext_ref[plane, block, pl.ds(row, length), :], back, 1)
            far = pltpu.roll(ext_ref[plane, block + 1, pl.ds(row, length), :], back, 1)
            return jnp.where(lane < LANES - shift, near, far)

        object_real, object_imag = patch(0), patch(1)
        intensity = jnp.zeros((length, length), F32)
        for number, pair in enumerate(pairs):
            reals, imags = [], []
            for m in pair:
                probe_real, probe_imag = probes_ref[m, 0], probes_ref[m, 1]
                reals.append((probe_real * object_real - probe_imag * object_imag).astype(BF16))
                imags.append((probe_real * object_imag + probe_imag * object_real).astype(BF16))
            wave = jnp.concatenate([jnp.concatenate(reals, axis=1), jnp.concatenate(imags, axis=1)], axis=0)
            half = dot(forward_ref[...], wave).astype(BF16)
            spectrum = dot(halves(half, len(pair)), adjoint_ref[...])
            for i in range(len(pair)):
                part = spectrum[i * length:(i + 1) * length]
                intensity += part[:, :length] * part[:, :length] + part[:, length:] * part[:, length:]
            if len(pairs) > 1:
                spectra_ref[number, :len(pair) * length] = spectrum
        amplitude = amplitude_ref[index].astype(F32)
        factor = 1.0 - amplitude * lax.rsqrt(jnp.maximum(intensity, FLOOR))
        term_real = jnp.zeros((length, length), F32)
        term_imag = jnp.zeros((length, length), F32)
        for number, pair in enumerate(pairs):
            if len(pairs) > 1:
                spectrum = spectra_ref[number, :len(pair) * length]
            reals, imags = [], []
            for i in range(len(pair)):
                part = spectrum[i * length:(i + 1) * length]
                reals.append((factor * part[:, :length]).astype(BF16))
                imags.append((factor * part[:, length:]).astype(BF16))
            chi = jnp.concatenate([jnp.concatenate(reals, axis=1), jnp.concatenate(imags, axis=1)], axis=0)
            half = dot(adjoint_ref[...], chi).astype(BF16)
            result = dot(halves(half, len(pair)), forward_ref[...])
            for i, m in enumerate(pair):
                real = result[i * length:(i + 1) * length, :length]
                imag = result[i * length:(i + 1) * length, length:]
                probe_real, probe_imag = probes_ref[m, 0], probes_ref[m, 1]
                term_real += probe_real * real + probe_imag * imag
                term_imag += probe_real * imag - probe_imag * real
                total_ref[m, 0] += object_real * real + object_imag * imag
                total_ref[m, 1] += object_real * imag - object_imag * real
        for plane, term in ((0, term_real), (1, term_imag)):
            moved = pltpu.roll(term, ahead, 1)
            canvas_ref[plane, block, pl.ds(row, length), :] += jnp.where(lane >= shift, moved, 0.0)
            canvas_ref[plane, block + 1, pl.ds(row, length), :] += jnp.where(lane < shift, moved, 0.0)

    @pl.loop(0, count, unroll=8 if count % 8 == 0 else 2)
    def _(index):
        step(index)


def gradients(n_mode, ext, probes, amplitudes, rows, columns, table):
    length = probes.shape[-1]
    vmem = pl.BlockSpec(memory_space=pltpu.VMEM)
    smem = pl.BlockSpec(memory_space=pltpu.SMEM)
    return pl.pallas_call(
        functools.partial(gradient_kernel, n_mode),
        out_shape=(
            jax.ShapeDtypeStruct(ext.shape, F32),
            jax.ShapeDtypeStruct(probes.shape, F32),
        ),
        in_specs=[smem, smem, vmem, vmem, vmem, vmem],
        out_specs=(vmem, vmem),
        scratch_shapes=[pltpu.VMEM(((n_mode + 1) // 2, 2 * length, 2 * length), F32)],
        compiler_params=pltpu.CompilerParams(vmem_limit_bytes=40 * 2**20),
        name="gradient",
    )(rows, columns, ext, probes, amplitudes, table)


def sum_kernel(n_tile, n_mode, canvas_ref, partial_ref, object_ref, probe_ref,
               landed, rim_out, rim_in, probe_in, probe_own, chunks_in, half_out, half_in,
               mode_send, mode_recv, rim_send, rim_recv, part_send, part_recv,
               scatter_send, scatter_recv, gather_send, gather_recv, twin_send, twin_recv):
    tile, mode = lax.axis_index("tile"), lax.axis_index("mode")
    strip = object_ref.shape[1]
    extent = canvas_ref.shape[2]
    margin = (extent - strip) // 2
    share = landed.shape[2]
    chunk = chunks_in.shape[1]
    reducers = probe_own.shape[0] // chunk
    group = n_tile // 2
    parity, member = lax.rem(tile, 2), tile // 2
    twin = tile + 1 - 2 * parity
    has_up, has_down = tile > 0, tile < n_tile - 1
    up, down = lax.max(tile - 1, 0), lax.min(tile + 1, n_tile - 1)
    partners = [lax.rem(mode + k, n_mode) for k in range(1, n_mode)]

    def peer(k):
        number = lax.rem(member + k, group)
        return number, 2 * number + parity

    barrier = pltpu.get_barrier_semaphore()
    for partner in partners:
        pl.semaphore_signal(barrier, inc=1, device_id=device(tile, partner), device_id_type=MESH)

    @pl.when(has_up)
    def _():
        pl.semaphore_signal(barrier, inc=1, device_id=device(up, mode), device_id_type=MESH)

    @pl.when(has_down)
    def _():
        pl.semaphore_signal(barrier, inc=1, device_id=device(down, mode), device_id_type=MESH)

    @pl.loop(1, group)
    def _(k):
        pl.semaphore_signal(barrier, inc=1, device_id=device(peer(k)[1], mode), device_id_type=MESH)

    signals = n_mode - 1 + group - 1 + has_up.astype(jnp.int32) + has_down.astype(jnp.int32)
    pl.semaphore_wait(barrier, signals)

    half = max(share // 2, 1)
    pieces = [(plane, low, half) for plane in range(2) for low in range(0, share, half)]

    sections = [(0, margin), (margin + strip, margin), (margin, strip)]

    def to_mode(p, section, plane):
        start, size = sections[section]
        return pltpu.make_async_remote_copy(
            src_ref=canvas_ref.at[plane, pl.ds(partners[p] * share, share), pl.ds(start, size), :],
            dst_ref=landed.at[p, plane, :, pl.ds(start, size), :],
            send_sem=mode_send.at[p, section, plane],
            recv_sem=mode_recv.at[p, section, plane],
            device_id=device(tile, partners[p]),
            device_id_type=MESH,
        )

    def part_to_mode(p):
        return pltpu.make_async_remote_copy(
            src_ref=partial_ref.at[partners[p]],
            dst_ref=probe_in.at[p],
            send_sem=part_send.at[p],
            recv_sem=part_recv.at[p],
            device_id=device(tile, partners[p]),
            device_id_type=MESH,
        )

    def rim(side, piece):
        plane, low, size = pieces[piece]
        return pltpu.make_async_remote_copy(
            src_ref=rim_out.at[side, plane, pl.ds(low, size)],
            dst_ref=rim_in.at[side, plane, pl.ds(low, size)],
            send_sem=rim_send.at[side, piece],
            recv_sem=rim_recv.at[side, piece],
            device_id=device(up if side == 0 else down, mode),
            device_id_type=MESH,
        )

    for p in range(n_mode - 1):
        part_to_mode(p).start()
    for plane in range(2):
        for section in (0, 1):
            for p in range(n_mode - 1):
                to_mode(p, section, plane).start()
    for plane in range(2):
        for p in range(n_mode - 1):
            to_mode(p, 2, plane).start()

    own_part = partial_ref[mode]
    for p in range(n_mode - 1):
        part_to_mode(p).wait_recv()
        own_part += probe_in[p]
    probe_own[...] = own_part.reshape(probe_own.shape)

    def rows_of(number):
        return pl.ds(pl.multiple_of(lax.rem(number, reducers) * chunk, chunk), chunk)

    def scatter(k):
        number, target = peer(k)
        return number, pltpu.make_async_remote_copy(
            src_ref=probe_own.at[rows_of(number), :],
            dst_ref=chunks_in.at[k - 1],
            send_sem=scatter_send.at[k - 1],
            recv_sem=scatter_recv.at[k - 1],
            device_id=device(target, mode),
            device_id_type=MESH,
        )

    @pl.loop(1, group)
    def _(k):
        number, copy = scatter(k)

        @pl.when(number < reducers)
        def _():
            copy.start()

    mine = pl.ds(mode * share, share)

    def sum_rims(plane):
        for section in (0, 1):
            start, size = sections[section]
            value = canvas_ref[plane, mine, start:start + size, :]
            for p in range(n_mode - 1):
                to_mode(p, section, plane).wait_recv()
                value += landed[p, plane, :, start:start + size, :]
            rim_out[section, plane] = value

    def send_rims(first, end):
        for piece in range(first, end):
            for section, sends in ((0, has_up), (1, has_down)):

                @pl.when(sends)
                def _():
                    rim(section, piece).start()

    count = len(pieces)
    sum_rims(0)
    send_rims(0, count // 2)
    sum_rims(1)

    to_twin = pltpu.make_async_remote_copy(
        src_ref=half_out, dst_ref=half_in, send_sem=twin_send, recv_sem=twin_recv,
        device_id=device(twin, mode), device_id_type=MESH,
    )

    def gather(k):
        return pltpu.make_async_remote_copy(
            src_ref=probe_ref.at[rows_of(member), :],
            dst_ref=probe_ref.at[rows_of(member), :],
            send_sem=gather_send.at[k - 1],
            recv_sem=gather_recv.at[k - 1],
            device_id=device(peer(k)[1], mode),
            device_id_type=MESH,
        )

    @pl.when(member < reducers)
    def _():
        @pl.loop(1, group)
        def _(k):
            scatter(k)[1].wait_recv()

        value = probe_own[rows_of(member), :]
        for k in range(group - 1):
            value += chunks_in[k]
        half_out[...] = value
        to_twin.start()

    send_rims(count // 2, 3 * count // 4)

    start, size = sections[2]
    for plane in range(2):
        value = canvas_ref[plane, mine, start:start + size, :]
        for p in range(n_mode - 1):
            to_mode(p, 2, plane).wait_recv()
            value += landed[p, plane, :, start:start + size, :]
        for k in range(share):
            object_ref[plane, :, k * LANES:(k + 1) * LANES] = value[k]

    @pl.when(member < reducers)
    def _():
        to_twin.wait_recv()
        probe_ref[rows_of(member), :] = half_out[...] + half_in[...]

        @pl.loop(1, group)
        def _(k):
            gather(k).start()

    send_rims(3 * count // 4, count)
    for piece, (plane, low, blocks) in enumerate(pieces):
        for side, gets, row in ((0, has_down, strip - margin), (1, has_up, 0)):

            @pl.when(gets)
            def _():
                rim(side, piece).wait_recv()
                for k in range(low, low + blocks):
                    object_ref[plane, row:row + margin, k * LANES:(k + 1) * LANES] += rim_in[side, plane, k]

    @pl.loop(1, group)
    def _(k):
        @pl.when(lax.rem(member + group - k, group) < reducers)
        def _():
            gather(k).wait_recv()

        number, copy = scatter(k)

        @pl.when(number < reducers)
        def _():
            copy.wait_send()

        @pl.when(member < reducers)
        def _():
            gather(k).wait_send()

    @pl.when(member < reducers)
    def _():
        to_twin.wait_send()

    for p in range(n_mode - 1):
        part_to_mode(p).wait_send()
        for section in range(3):
            for plane in range(2):
                to_mode(p, section, plane).wait_send()
    for section, sends in ((0, has_up), (1, has_down)):

        @pl.when(sends)
        def _():
            for piece in range(count):
                rim(section, piece).wait_send()


def sum_gradients(n_tile, n_mode, canvas, partial, margin):
    planes, blocks, extent, _ = canvas.shape
    length = partial.shape[-1]
    share = blocks // n_mode
    strip = extent - 2 * margin
    peers = max(n_mode - 1, 1)
    pieces = planes * (share // max(share // 2, 1))
    chunk = max(2 * length // (n_tile // 2), 8)
    dma = pltpu.SemaphoreType.DMA
    vmem = pl.BlockSpec(memory_space=pltpu.VMEM)
    others = n_tile // 2 - 1
    object_grad, probe_grad = pl.pallas_call(
        functools.partial(sum_kernel, n_tile, n_mode),
        out_shape=(
            jax.ShapeDtypeStruct((planes, strip, share * LANES), F32),
            jax.ShapeDtypeStruct((2 * length, length), F32),
        ),
        in_specs=[vmem, vmem],
        out_specs=(vmem, vmem),
        scratch_shapes=[
            pltpu.VMEM((peers, planes, share, extent, LANES), F32),
            pltpu.VMEM((2, planes, share, margin, LANES), F32),
            pltpu.VMEM((2, planes, share, margin, LANES), F32),
            pltpu.VMEM((peers, 2, length, length), F32),
            pltpu.VMEM((2 * length, length), F32),
            pltpu.VMEM((others, chunk, length), F32),
            pltpu.VMEM((chunk, length), F32),
            pltpu.VMEM((chunk, length), F32),
            dma((peers, 3, planes)), dma((peers, 3, planes)),
            dma((2, pieces)), dma((2, pieces)),
            dma((peers,)), dma((peers,)),
            dma((others,)), dma((others,)), dma((others,)), dma((others,)), dma, dma,
        ],
        compiler_params=pltpu.CompilerParams(
            collective_id=1, has_side_effects=True, vmem_limit_bytes=40 * 2**20
        ),
        name="sums",
    )(canvas, partial)
    return object_grad, probe_grad.reshape(1, 2, length, length)


def solution(mesh):
    n_tile, n_mode = mesh.shape["tile"], mesh.shape["mode"]

    def body(object_wave, probe, amplitudes, rows, columns):
        held = exchange_halo(n_tile, n_mode, object_wave, probe, amplitudes, rows, columns)
        canvas, partial = gradients(n_mode, *held)
        return sum_gradients(n_tile, n_mode, canvas, partial, probe.shape[-1] // 2)

    placed = (
        P(None, "tile", None),
        P("mode", None, None, None),
        P("tile", None, None),
        P("tile"),
        P("tile"),
    )
    return jax.shard_map(
        body,
        mesh=mesh,
        in_specs=placed,
        out_specs=(P(None, "tile", "mode"), P("mode", None, None, None)),
        check_vma=False,
    )
```
